256 devices in a mesh: leaf: 64 (over z, y, core), level: 4 (over x).
Axes of the slice: x: 4, y: 4, z: 8, core: 2. Of those that a mesh axis runs over, the one named last changes fastest.
Arguments:
- vectors: bfloat16 [2048, 32, 128], P('leaf'), may hold values from -6 to 6
- leaf_basis: bfloat16 [2048, 32, 128], P('leaf'), may hold values from -0.5 to 0.5
- transfer: bfloat16 [2048, 32, 32], P('leaf'), may hold values from -0.1875 to 0.1875
- nearfield_source_leaf: int32 [2048, 16], P('leaf', 'level'), may hold values from 0 to 2047, as said below
- near_count: int32 [2048], P('leaf'), may hold values from 1 to 16
- nearfield_block_matrix: bfloat16 [2048, 16, 128, 128], P('leaf', 'level'), may hold values from -0.25 to 0.25
- far_source: int32 [2048, 16], P('leaf', 'level'), may hold values from 0 to 2047, as said below
- far_count: int32 [2048], P('leaf'), may hold values from 1 to 16
- far_block: bfloat16 [2048, 16, 1024], P('leaf', 'level'), may hold values from -0.75 to 0.75
- top_source: int32 [64, 16], P('leaf', 'level'), may hold values from 0 to 63
- top_count: int32 [64], P('leaf'), may hold values from 1 to 16
- top_block: bfloat16 [64, 16, 1024], P('leaf', 'level'), may hold values from -1.5 to 1.5
Outputs:
- product: bfloat16 [2048, 32, 128], P('leaf', 'level')
The draws below stay inside these ranges and needn't reach their ends.
Inputs may be any that keep to these rules, and one draw needn't show every extreme that they name: `nearfield_source_leaf`: each near-field source leaf lies within 32 leaves of its target leaf's index. `far_source`: each coupling source leaf lies within 32 leaves of its target leaf's index.
All inputs are finite; a program needn't handle non-finite values.
Results may differ from the reference program's by a relative error of at most 0.0036.
Values may be sent and summed in bfloat16 or wider, within the bound.
No kernel may reach another device: no remote copies, remote signals or barrier semaphores. Data moves between devices by JAX's collectives and lax.ppermute only.
A program may use at most 64 MiB of HBM per device.

```python
import jax
import jax.numpy as jnp
from jax import lax

LEAF = 128
RANK = 32
RHS = 32
NEAR = 16
LEAF_FAR = 16
TOP_FAR = 16
LEAF_DEV = 32
NLEAF = 2048
NTOP = 64


def window_sources(key, slots):
    target = jnp.arange(NLEAF, dtype=jnp.int32)[:, None]
    offset = jax.random.randint(key, (NLEAF, slots), -LEAF_DEV, LEAF_DEV + 1, dtype=jnp.int32)
    first = target + offset
    interior_terms = (first >= 0) & (first < NLEAF)
    return jnp.where(interior_terms, first, target - offset).astype(jnp.int32)


def draw_nearfield_source_leaf(key, part):
    key = jax.random.fold_in(key, 11)
    return window_sources(key, NEAR)


def draw_far_source(key, part):
    key = jax.random.fold_in(key, 23)
    return window_sources(key, LEAF_FAR)


def place_ends(values, rng, low, top_value):
    longest = values.shape.index(max(values.shape))
    spots = []
    for shift in (0, 1):
        where = [jax.random.randint(jax.random.fold_in(rng, axis), (), 0, length) for axis, length in enumerate(values.shape)]
        where[longest] = (where[longest] + shift) % values.shape[longest]
        spots.append(tuple(where))
    return values.at[spots[0]].set(low).at[spots[1]].set(top_value)


def level_of(own_key, extent, cuts, low, high):
    gain = 1.0
    for axis_at, shards_of in cuts:
        heights = jax.random.uniform(jax.random.fold_in(jax.random.fold_in(own_key, 6), axis_at), (shards_of,), jnp.float32, low / len(cuts), high / len(cuts))
        gain = gain * jnp.repeat(jnp.exp(heights), extent[axis_at] // shards_of).reshape((-1,) + (1,) * (len(extent) - 1 - axis_at))
    return gain


def scatter_about(own_key, shape, scale, reach, shards=(), held_as=jnp.bfloat16):
    level = level_of(own_key, shape, shards, -0.22, 0.18) if shards else 1.0
    values = jax.random.normal(own_key, shape, jnp.float32) * scale * level
    return jnp.minimum(jnp.maximum(values, -reach), reach).astype(held_as)


def setup_inputs(seed: int = 0) -> dict:
    key_of = jax.random.split(jax.random.key(seed), 13)
    vectors = scatter_about(key_of[0], (NLEAF, RHS, LEAF), 1.0, 6.0, ((0, 64),))
    leaf_basis = scatter_about(key_of[1], (NLEAF, RANK, LEAF), LEAF ** -0.5, 0.5, ((0, 64),))
    transfer = scatter_about(key_of[2], (NLEAF, RANK, RANK), (RANK * LEAF_DEV) ** -0.5, 0.1875, ((0, 64),))
    nearfield_source_leaf = draw_nearfield_source_leaf(jax.random.fold_in(key_of[12], 71), 0)
    near_count = place_ends(jax.random.randint(key_of[4], (NLEAF,), 1, NEAR + 1), jax.random.fold_in(key_of[4], 1), 1, NEAR).astype(jnp.int32)
    nearfield_block_matrix = scatter_about(key_of[5], (NLEAF, NEAR, LEAF, LEAF), (LEAF * NEAR // 4) ** -0.5, 0.25, ((0, 64), (1, 4)))
    far_source = draw_far_source(jax.random.fold_in(key_of[12], 71), 0)
    far_count = place_ends(jax.random.randint(key_of[7], (NLEAF,), 1, LEAF_FAR + 1), jax.random.fold_in(key_of[7], 1), 1, LEAF_FAR).astype(jnp.int32)
    far_block = scatter_about(key_of[8], (NLEAF, LEAF_FAR, RANK * RANK), (RANK * 2) ** -0.5, 0.75, ((0, 64), (1, 4)))
    top_source = place_ends(jax.random.randint(key_of[9], (NTOP, TOP_FAR), 0, NTOP), jax.random.fold_in(key_of[9], 1), 0, NTOP - 1).astype(jnp.int32)
    top_count = place_ends(jax.random.randint(key_of[10], (NTOP,), 1, TOP_FAR + 1), jax.random.fold_in(key_of[10], 1), 1, TOP_FAR).astype(jnp.int32)
    top_block = scatter_about(key_of[11], (NTOP, TOP_FAR, RANK * RANK), (RANK * TOP_FAR // LEAF_DEV) ** -0.5, 1.5, ((0, 64), (1, 4)))
    return dict(vectors=vectors, leaf_basis=leaf_basis, transfer=transfer, nearfield_source_leaf=nearfield_source_leaf, near_count=near_count, nearfield_block_matrix=nearfield_block_matrix, far_source=far_source, far_count=far_count, far_block=far_block, top_source=top_source, top_count=top_count, top_block=top_block)


def reference(vectors, leaf_basis, transfer, nearfield_source_leaf, near_count, nearfield_block_matrix, far_source, far_count, far_block, top_source, top_count, top_block):
    fvec = vectors.astype(jnp.float32)
    fbasis = leaf_basis.astype(jnp.float32)
    coef = jnp.einsum("nrp,nkp->nkr", fvec, fbasis).astype(jnp.bfloat16)
    ftrans = transfer.astype(jnp.float32)
    root_coef = jnp.einsum("tnab,tnbr->tar", ftrans.reshape(NTOP, LEAF_DEV, RANK, RANK), coef.astype(jnp.float32).reshape(NTOP, LEAF_DEV, RANK, RHS)).astype(jnp.bfloat16)

    near_live = (jnp.arange(NEAR, dtype=jnp.int32)[None, :] < near_count[:, None]).astype(jnp.float32)

    def near_group(args):
        sources, blocks, active = args
        collected_vectors = fvec[sources] * active[:, :, None, None]
        return jnp.einsum("nsrq,nspq->nrp", collected_vectors, blocks.astype(jnp.float32))

    near_sum = lax.map(near_group, (nearfield_source_leaf.reshape(NTOP, LEAF_DEV, NEAR), nearfield_block_matrix.reshape(NTOP, LEAF_DEV, NEAR, LEAF, LEAF), near_live.reshape(NTOP, LEAF_DEV, NEAR)))
    near_sum = near_sum.reshape(NLEAF, RHS, LEAF)

    far_live = (jnp.arange(LEAF_FAR, dtype=jnp.int32)[None, :] < far_count[:, None]).astype(jnp.float32)
    far_src = coef.astype(jnp.float32)[far_source] * far_live[:, :, None, None]
    far_sum = jnp.einsum("nsab,nsbr->nar", far_block.astype(jnp.float32).reshape(NLEAF, LEAF_FAR, RANK, RANK), far_src)

    top_live = (jnp.arange(TOP_FAR, dtype=jnp.int32)[None, :] < top_count[:, None]).astype(jnp.float32)
    top_src = root_coef.astype(jnp.float32)[top_source] * top_live[:, :, None, None]
    top_sum = jnp.einsum("tsab,tsbr->tar", top_block.astype(jnp.float32).reshape(NTOP, TOP_FAR, RANK, RANK), top_src)

    lowered = jnp.einsum("tnab,tar->tnbr", ftrans.reshape(NTOP, LEAF_DEV, RANK, RANK), top_sum, precision=lax.Precision.HIGHEST)
    down = far_sum + lowered.reshape(NLEAF, RANK, RHS)
    result = near_sum + jnp.einsum("nkr,nkp->nrp", down, fbasis, precision=lax.Precision.HIGHEST)
    return result.astype(jnp.bfloat16)
```

```python
import jax
import jax.numpy as jnp
from jax import lax
from jax.experimental import pallas as pl
from jax.experimental.pallas import tpu as pltpu
from jax.sharding import PartitionSpec as P

BF = jnp.bfloat16
F32 = jnp.float32
LEAVES = 32
GROUP = 4
PACKED = LEAVES + LEAVES // GROUP
ROWS = 8
STEPS = 4
PER_STEP = LEAVES // STEPS
NONE = 3 * LEAVES


def dot_nt(a, b):
    return lax.dot_general(a, b, (((1,), (1,)), ((), ())), preferred_element_type=F32)


def dot_nn(a, b):
    return lax.dot_general(a, b, (((1,), (0,)), ((), ())), preferred_element_type=F32)


def two_terms(value):
    high = value.astype(BF)
    return high, (value - high.astype(F32)).astype(BF)


def coef_kernel(level, vectors, basis, transfer, packed, root, wide):
    packed[0:LEAVES] = vectors[...]
    total = jnp.zeros((32, 32), F32)
    for g in range(LEAVES // GROUP):
        pieces = []
        for m in range(GROUP):
            i = g * GROUP + m
            c = dot_nt(vectors[i], basis[i]).astype(BF)
            total = total + dot_nt(c, transfer[i])
            pieces.append(c)
        packed[LEAVES + g] = jnp.concatenate(pieces, axis=1)
    wide[...] = jnp.concatenate([total] * GROUP, axis=1)
    first = pl.multiple_of(level[0] * ROWS, ROWS)
    root[...] = wide[pl.ds(first, ROWS), :].astype(BF)


def near_far_kernel(
    level, near_at, far_at, top_at, own, before, after, blocks, far, basis, kept, out1, out2, out3, vtab, ctab, prod
):
    step = pl.program_id(0)

    @pl.when(step == 0)
    def _():
        for n, part in enumerate((before, own, after)):
            vtab[n * LEAVES : (n + 1) * LEAVES] = part[0:LEAVES]
            lane = lax.broadcasted_iota(jnp.int32, (32, 128), 1) // 32
            for g in range(LEAVES // GROUP):
                tile = part[LEAVES + g].astype(F32)
                turned = [tile] + [pltpu.roll(tile, 32 * k, 1) for k in range(1, GROUP)]
                for m in range(GROUP):
                    v = turned[(0 - m) % GROUP]
                    for k in range(1, GROUP):
                        v = jnp.where(lane == k, turned[(k - m) % GROUP], v)
                    ctab[n * LEAVES + g * GROUP + m] = v.astype(BF)
        vtab[NONE] = jnp.zeros((32, 128), BF)
        ctab[NONE] = jnp.zeros((32, 128), BF)
        top = far[LEAVES]
        row = lax.broadcasted_iota(jnp.int32, (16, 128), 0)
        names = jnp.full((16, 128), -1, jnp.int32)
        for s in range(4):
            names = jnp.where(row == s, top_at[s], names)
        for out in (out1, out2, out3):
            out[LEAVES // 2 + 2] = names.astype(F32).astype(BF)
            out[LEAVES // 2] = top[0:16]
            out[LEAVES // 2 + 1] = top[16:32]

    me = level[0]
    lane = lax.broadcasted_iota(jnp.int32, (32, 128), 1) // 32
    for j in range(PER_STEP):
        i = step * PER_STEP + j
        value = jnp.zeros((32, 128), F32)
        for s in range(4):
            value = value + dot_nt(vtab[near_at[i * 4 + s]], blocks[j, s])
        c = ctab[far_at[i * 4]]
        for s in range(1, 4):
            c = jnp.where(lane == s, ctab[far_at[i * 4 + s]], c)
        down = dot_nt(c, far[i])
        high, low = two_terms(down)
        b = basis[i]
        value = value + dot_nn(high, b) + dot_nn(low, b)
        prod[j] = value
    for h in range(PER_STEP // 2):
        pair = step * (PER_STEP // 2) + h

        def rows(k):
            at = pl.multiple_of(lax.rem(me + k, 4) * ROWS, ROWS)
            return jnp.concatenate([prod[2 * h, pl.ds(at, ROWS), :], prod[2 * h + 1, pl.ds(at, ROWS), :]], axis=0)

        kept[pair] = rows(0)
        for k, out in ((1, out1), (2, out2), (3, out3)):
            out[pair] = rows(k).astype(BF)


def top_operator_kernel(transfer, basis, operator):
    for i in range(LEAVES):
        high, low = two_terms(dot_nn(transfer[i], basis[i]))
        operator[0:32, i * 128 : (i + 1) * 128] = high
        operator[32:64, i * 128 : (i + 1) * 128] = low


def final_kernel(top_at, roots, far, operator, kept, got1, got2, got3, out):
    lane = lax.broadcasted_iota(jnp.int32, (ROWS, 128), 1) // 32
    total = jnp.zeros((ROWS, 32), F32)
    for k, got in enumerate((None, got1, got2, got3)):
        c = jnp.zeros((ROWS, 128), F32)
        for s in range(4):
            at = top_at[k * 4 + s]
            row = roots[jnp.maximum(at, 0)].astype(F32)
            c = jnp.where((lane == s) & (at >= 0), row, c)
        c = c.astype(BF)
        if got is None:
            total = total + dot_nt(c, far[0])
        else:
            total = total + dot_nt(c, jnp.concatenate([got[LEAVES // 2], got[LEAVES // 2 + 1]], axis=0))
    high, low = two_terms(total)
    lhs = jnp.concatenate([high, low], axis=1)
    for h in range(LEAVES // 2):
        value = kept[h] + got1[h].astype(F32) + got2[h].astype(F32) + got3[h].astype(F32)
        halves = []
        for n in range(2):
            w = operator[:, (2 * h + n) * 128 : (2 * h + n + 1) * 128]
            t = dot_nn(lhs, jnp.concatenate([w[0:32], w[0:32]], axis=0)) + dot_nn(high, w[32:64])
            halves.append(t)
        out[h] = (value + jnp.concatenate(halves, axis=0)).astype(BF)


def whole(shape):
    return pl.BlockSpec(shape, lambda *_: (0,) * len(shape))


SMEM = pl.BlockSpec(memory_space=pltpu.SMEM)


def per_device(
    vectors,
    leaf_basis,
    transfer,
    nearfield_source_leaf,
    near_count,
    nearfield_block_matrix,
    far_source,
    far_count,
    far_block,
    top_source,
    top_count,
    top_block,
):
    level = lax.axis_index("level")
    leaf = lax.axis_index("leaf")
    level_in = level.reshape(1).astype(jnp.int32)
    packed, root = pl.pallas_call(
        coef_kernel,
        out_shape=(
            jax.ShapeDtypeStruct((PACKED, 32, 128), BF),
            jax.ShapeDtypeStruct((ROWS, 128), BF),
        ),
        in_specs=[SMEM, whole((32, 32, 128)), whole((32, 32, 128)), whole((32, 32, 32))],
        out_specs=(whole((PACKED, 32, 128)), whole((ROWS, 128))),
        scratch_shapes=[pltpu.VMEM((32, 128), F32)],
        name="coefficients",
    )(level_in, vectors, leaf_basis, transfer)

    up = [(n, n + 1) for n in range(63)]
    down = [(n + 1, n) for n in range(63)]
    before = lax.ppermute(packed, "leaf", up)
    after = lax.ppermute(packed, "leaf", down)
    roots = lax.all_to_all(
        jnp.broadcast_to(root[None], (64, ROWS, 128)), "leaf", 0, 0, tiled=True
    )

    slot = level * 4 + jnp.arange(4, dtype=jnp.int32)
    shift = LEAVES - leaf * LEAVES
    near_at = jnp.where(slot[None] < near_count[:, None], nearfield_source_leaf + shift, NONE).reshape(-1)
    far_at = jnp.where(slot[None] < far_count[:, None], far_source + shift, NONE).reshape(-1)
    couplings = jnp.concatenate([far_block, top_block], axis=0)
    couplings = couplings.reshape(LEAVES + 1, 4, 32, 32).transpose(0, 2, 1, 3).reshape(LEAVES + 1, 32, 128)

    operator = pl.pallas_call(
        top_operator_kernel,
        out_shape=jax.ShapeDtypeStruct((64, LEAVES * 128), BF),
        in_specs=[whole((32, 32, 32)), whole((32, 32, 128))],
        out_specs=whole((64, LEAVES * 128)),
        name="top_operator",
    )(transfer, leaf_basis)

    parts = LEAVES // 2
    top_live = jnp.where(slot < top_count[0], top_source[0], -1)
    sent = jax.ShapeDtypeStruct((parts + 3, 16, 128), BF)
    kept, *outs = pl.pallas_call(
        near_far_kernel,
        grid=(STEPS,),
        out_shape=(jax.ShapeDtypeStruct((parts, 16, 128), F32), sent, sent, sent),
        in_specs=[
            SMEM,
            SMEM,
            SMEM,
            SMEM,
            whole((PACKED, 32, 128)),
            whole((PACKED, 32, 128)),
            whole((PACKED, 32, 128)),
            pl.BlockSpec((PER_STEP, 4, 128, 128), lambda n: (n, 0, 0, 0)),
            whole((LEAVES + 1, 32, 128)),
            whole((LEAVES, 32, 128)),
        ],
        out_specs=(whole((parts, 16, 128)),) + (whole((parts + 3, 16, 128)),) * 3,
        scratch_shapes=[
            pltpu.VMEM((NONE + 1, 32, 128), BF),
            pltpu.VMEM((NONE + 1, 32, 128), BF),
            pltpu.VMEM((PER_STEP, 32, 128), F32),
        ],
        name="near_far",
    )(level_in, near_at, far_at, top_live, packed, before, after, nearfield_block_matrix, couplings, leaf_basis)

    got = []
    for k, out in zip((1, 2, 3), outs):
        got.append(lax.ppermute(out, "level", [(n, (n + k) % 4) for n in range(4)]))

    top_at = jnp.concatenate(
        [top_live] + [part[parts + 2, 0:4, 0].astype(jnp.int32) for part in got]
    )
    result = pl.pallas_call(
        final_kernel,
        out_shape=jax.ShapeDtypeStruct((parts, 16, 128), BF),
        grid=(1,),
        in_specs=[
            SMEM,
            whole((64, ROWS, 128)),
            pl.BlockSpec((1, 32, 128), lambda n: (LEAVES, 0, 0)),
            whole((64, LEAVES * 128)),
            whole((parts, 16, 128)),
            whole((parts + 3, 16, 128)),
            whole((parts + 3, 16, 128)),
            whole((parts + 3, 16, 128)),
        ],
        out_specs=whole((parts, 16, 128)),
        name="final",
    )(top_at, roots, couplings, operator, kept, *got)
    return result.reshape(LEAVES, ROWS, 128)


def solution(mesh):
    placed = (
        P("leaf", None, None),
        P("leaf", None, None),
        P("leaf", None, None),
        P("leaf", "level"),
        P("leaf"),
        P("leaf", "level", None, None),
        P("leaf", "level"),
        P("leaf"),
        P("leaf", "level", None),
        P("leaf", "level"),
        P("leaf"),
        P("leaf", "level", None),
    )
    return jax.shard_map(
        per_device, mesh=mesh, in_specs=placed, out_specs=P("leaf", "level", None), check_vma=False
    )
```

```python
import jax
import jax.numpy as jnp
from jax import lax
from jax.experimental import pallas as pl
from jax.experimental.pallas import tpu as pltpu
from jax.sharding import PartitionSpec as P

BF = jnp.bfloat16
F32 = jnp.float32
LEAVES = 32
ROOTS = 64
GROUP = 4
PACKED = LEAVES + LEAVES // GROUP
ROWS = 8
STEPS = 2
PER_STEP = LEAVES // STEPS
AHEAD = 2
NONE = 3 * LEAVES


def dot_nt(a, b):
    return lax.dot_general(a, b, (((1,), (1,)), ((), ())), preferred_element_type=F32)


def dot_nn(a, b):
    return lax.dot_general(a, b, (((1,), (0,)), ((), ())), preferred_element_type=F32)


def two_terms(value):
    high = value.astype(BF)
    return high, (value - high.astype(F32)).astype(BF)


def coef_kernel(level, vectors, basis_in, transfer_in, packed, basis, transfer, spread, wide, sems):
    copies = [
        pltpu.make_async_copy(vectors, packed.at[0:LEAVES], sems.at[0]),
        pltpu.make_async_copy(basis_in, basis, sems.at[1]),
        pltpu.make_async_copy(transfer_in, transfer, sems.at[2]),
    ]
    for copy in copies:
        copy.start()
    for copy in copies:
        copy.wait()
    total = jnp.zeros((32, 32), F32)
    for g in range(LEAVES // GROUP):
        pieces = []
        for m in range(GROUP):
            i = g * GROUP + m
            c = dot_nt(packed[i], basis[i]).astype(BF)
            total = total + dot_nt(c, transfer[i])
            pieces.append(c)
        packed[LEAVES + g] = jnp.concatenate(pieces, axis=1)
    wide[...] = jnp.concatenate([total] * GROUP, axis=1)
    root = wide[pl.ds(pl.multiple_of(level[0] * ROWS, ROWS), ROWS), :].astype(BF)
    twice = jnp.concatenate([root, root], axis=0)
    for t in range(ROOTS // 2):
        spread[t] = twice


def couplings(rows4, lane, row):
    x = jnp.concatenate([rows4[:, p * 128 : (p + 1) * 128] for p in range(8)], axis=0)
    out = x
    for d in range(1, 4):
        turned = jnp.where(row < 4 - d, pltpu.roll(x, 32 - d, 0), pltpu.roll(x, 4 - d, 0))
        out = jnp.where((row + d) % 4 == lane, pltpu.roll(turned, 32 * d, 1), out)
    return out


def near_far_kernel(
    level,
    leaf,
    near_source_in,
    near_count_in,
    far_source_in,
    far_count_in,
    top_source_in,
    top_count,
    own,
    before,
    after,
    blocks_in,
    far_in,
    top_in,
    basis,
    kept,
    out1,
    out2,
    out3,
    top_own,
    names_own,
    near_source,
    near_count,
    far_source,
    far_count,
    top_source,
    vtab,
    ctab,
    prod,
    terms,
    blocks,
    far,
    top,
    sems,
):
    def stream(n):
        part = pl.ds(n * PER_STEP, PER_STEP)
        return pltpu.make_async_copy(blocks_in.at[part], blocks.at[part], sems.at[n])

    small = [
        pltpu.make_async_copy(a, b, sems.at[STEPS + n])
        for n, (a, b) in enumerate(
            (
                (near_source_in, near_source),
                (near_count_in, near_count),
                (far_source_in, far_source),
                (far_count_in, far_count),
                (top_source_in, top_source),
                (top_in, top),
                (far_in, far),
            )
        )
    ]
    for copy in small:
        copy.start()
    for n in range(AHEAD):
        stream(n).start()
    lane = lax.broadcasted_iota(jnp.int32, (32, 128), 1) // 32
    row = lax.broadcasted_iota(jnp.int32, (32, 128), 0) % 4
    for n, part in enumerate((before, own, after)):
        vtab[n * LEAVES : (n + 1) * LEAVES] = part[0:LEAVES]
        for g in range(LEAVES // GROUP):
            tile = part[LEAVES + g].astype(F32)
            turned = [tile] + [pltpu.roll(tile, 32 * k, 1) for k in range(1, GROUP)]
            for m in range(GROUP):
                v = turned[(0 - m) % GROUP]
                for k in range(1, GROUP):
                    v = jnp.where(lane == k, turned[(k - m) % GROUP], v)
                ctab[n * LEAVES + g * GROUP + m] = v.astype(BF)
    vtab[NONE] = jnp.zeros((32, 128), BF)
    ctab[NONE] = jnp.zeros((32, 128), BF)

    me = level[0]
    first = me * 4
    shift = LEAVES - leaf[0] * LEAVES
    for copy in small:
        copy.wait()
    top_f = couplings(top[0].astype(F32), lane, row).astype(BF)
    top_own[...] = top_f
    row8 = lax.broadcasted_iota(jnp.int32, (16, 128), 0)
    names = jnp.full((16, 128), -1, jnp.int32)
    for s in range(4):
        names = jnp.where(row8 == s, jnp.where(first + s < top_count[0], top_source[0, s], -1), names)
    names_own[...] = names[0:8]
    names = names.astype(F32).astype(BF)
    for out in (out1, out2, out3):
        out[LEAVES // 2] = top_f[0:16]
        out[LEAVES // 2 + 1] = top_f[16:32]
        out[LEAVES // 2 + 2] = names

    same = lax.broadcasted_iota(jnp.int32, (128, 128), 0) // 32 == lax.broadcasted_iota(jnp.int32, (128, 128), 1) // 32
    for g in range(LEAVES // GROUP):
        chosen = []
        matrices = []
        for m in range(GROUP):
            i = g * GROUP + m
            far_at = [jnp.where(first + s < far_count[i], far_source[s, i] + shift, NONE) for s in range(4)]
            c = ctab[far_at[0]]
            for s in range(1, 4):
                c = jnp.where(lane == s, ctab[far_at[s]], c)
            chosen.append(c)
            matrices.append(couplings(far[i].astype(F32), lane, row).astype(BF))
        down = dot_nt(jnp.concatenate(chosen, axis=0), jnp.concatenate(matrices, axis=0))
        terms[g] = jnp.concatenate(two_terms(jnp.where(same, down, 0.0)), axis=1)

    @pl.loop(0, STEPS)
    def _(step):
        stream(step).wait()

        @pl.when(step + AHEAD < STEPS)
        def _():
            stream(step + AHEAD).start()

        for h in range(PER_STEP // GROUP):
            g = step * (PER_STEP // GROUP) + h
            b = basis[pl.ds(g * GROUP, GROUP)].reshape(GROUP * 32, 128)
            value = dot_nn(terms[g], jnp.concatenate([b, b], axis=0))
            for m in range(GROUP):
                i = g * GROUP + m
                near_at = [jnp.where(first + s < near_count[i], near_source[s, i] + shift, NONE) for s in range(4)]
                total = value[m * 32 : m * 32 + 32]
                for s in range(0, 4, 2):
                    lhs = jnp.concatenate([vtab[near_at[s]], vtab[near_at[s + 1]]], axis=1)
                    rhs = jnp.concatenate([blocks[i, s], blocks[i, s + 1]], axis=1)
                    total = total + dot_nt(lhs, rhs)
                prod[h * GROUP + m] = total
            for m in range(0, GROUP, 2):
                pair = (step * PER_STEP + h * GROUP + m) // 2

                def rows(k):
                    at = pl.multiple_of(lax.rem(me + k, 4) * ROWS, ROWS)
                    n = h * GROUP + m
                    return jnp.concatenate([prod[n, pl.ds(at, ROWS), :], prod[n + 1, pl.ds(at, ROWS), :]], axis=0)

                kept[pair] = rows(0)
                for k, out in ((1, out1), (2, out2), (3, out3)):
                    out[pair] = rows(k).astype(BF)


def top_operator_kernel(transfer, basis, operator):
    for i in range(LEAVES):
        high, low = two_terms(dot_nn(transfer[i], basis[i]))
        operator[0:32, i * 128 : (i + 1) * 128] = high
        operator[32:64, i * 128 : (i + 1) * 128] = low


def final_kernel(roots, operator, kept, top_own, names_own, got1, got2, got3, out, names_v, names_s, sem):
    others = (got1, got2, got3)
    names_v[0:ROWS] = names_own[...]
    for k, got in enumerate(others):
        names_v[(k + 1) * ROWS : (k + 2) * ROWS] = got[LEAVES // 2 + 2].astype(F32)[0:ROWS].astype(jnp.int32)
    copy = pltpu.make_async_copy(names_v, names_s, sem)
    copy.start()
    for h in range(LEAVES // 2):
        kept[h] = kept[h] + got1[h].astype(F32) + got2[h].astype(F32) + got3[h].astype(F32)
    lane = lax.broadcasted_iota(jnp.int32, (ROWS, 128), 1) // 32
    total = jnp.zeros((ROWS, 32), F32)
    copy.wait()
    for k in range(4):
        c = jnp.zeros((ROWS, 128), F32)
        for s in range(4):
            at = names_s[k * ROWS + s, 0]
            c = jnp.where((lane == s) & (at >= 0), roots[jnp.maximum(at, 0)].astype(F32), c)
        c = c.astype(BF)
        if k == 0:
            total = total + dot_nt(c, top_own[...])
        else:
            got = others[k - 1]
            total = total + dot_nt(c, jnp.concatenate([got[LEAVES // 2], got[LEAVES // 2 + 1]], axis=0))
    high, low = two_terms(total)
    lhs = jnp.concatenate([high, low, high], axis=1)
    for h in range(LEAVES // 2):
        w = operator[:, h * 256 : (h + 1) * 256]
        t = dot_nn(lhs, jnp.concatenate([w[0:32], w[0:32], w[32:64]], axis=0))
        out[h] = (kept[h] + jnp.concatenate([t[:, 0:128], t[:, 128:256]], axis=0)).astype(BF)


SMEM = pl.BlockSpec(memory_space=pltpu.SMEM)
VMEM = pl.BlockSpec(memory_space=pltpu.VMEM)
HBM = pl.BlockSpec(memory_space=pltpu.HBM)
LIMIT = 16 * 1024 * 1024


def held(value):
    return pltpu.with_memory_space_constraint(value, pltpu.VMEM)


def stays(value):
    return pltpu.with_memory_space_constraint(value, pltpu.HBM)


def params(flops):
    return dict(
        compiler_params=pltpu.CompilerParams(vmem_limit_bytes=LIMIT),
        cost_estimate=pl.CostEstimate(flops=flops, bytes_accessed=1 << 20, transcendentals=0),
    )


def gathered(spread):
    return lax.all_to_all(spread, "leaf", 0, 0, tiled=True)


def per_device(
    vectors,
    leaf_basis,
    transfer,
    nearfield_source_leaf,
    near_count,
    nearfield_block_matrix,
    far_source,
    far_count,
    far_block,
    top_source,
    top_count,
    top_block,
):
    level = lax.axis_index("level").astype(jnp.int32).reshape(1)
    leaf = lax.axis_index("leaf").astype(jnp.int32).reshape(1)
    packed, basis, carried, spread = pl.pallas_call(
        coef_kernel,
        out_shape=(
            pltpu.VMEM((PACKED, 32, 128), BF),
            pltpu.VMEM((LEAVES, 32, 128), BF),
            pltpu.VMEM((LEAVES, 32, 32), BF),
            pltpu.VMEM((ROOTS // 2, 2 * ROWS, 128), BF),
        ),
        in_specs=[SMEM] + [HBM] * 3,
        out_specs=(VMEM,) * 4,
        scratch_shapes=[pltpu.VMEM((32, 128), F32), pltpu.SemaphoreType.DMA((3,))],
        name="coefficients",
        **params(1 << 24),
    )(level, stays(vectors), stays(leaf_basis), stays(transfer))

    before = lax.ppermute(packed, "leaf", [(n, n + 1) for n in range(63)])
    after = lax.ppermute(packed, "leaf", [(n + 1, n) for n in range(63)])
    roots = gathered(spread.reshape(ROOTS, ROWS, 128))

    operator = pl.pallas_call(
        top_operator_kernel,
        out_shape=pltpu.VMEM((64, LEAVES * 128), BF),
        in_specs=[VMEM, VMEM],
        out_specs=VMEM,
        name="top_operator",
        **params(1 << 24),
    )(held(carried), held(basis))

    parts = LEAVES // 2
    sent = pltpu.VMEM((parts + 3, 16, 128), BF)
    kept, out1, out2, out3, top_own, names_own = pl.pallas_call(
        near_far_kernel,
        out_shape=(
            pltpu.VMEM((parts, 16, 128), F32),
            sent,
            sent,
            sent,
            pltpu.VMEM((32, 128), BF),
            pltpu.VMEM((ROWS, 128), jnp.int32),
        ),
        in_specs=[SMEM] * 2 + [HBM] * 5 + [SMEM] + [VMEM] * 3 + [HBM] * 3 + [VMEM],
        out_specs=(VMEM,) * 6,
        scratch_shapes=[
            pltpu.SMEM((4, LEAVES), jnp.int32),
            pltpu.SMEM((LEAVES,), jnp.int32),
            pltpu.SMEM((4, LEAVES), jnp.int32),
            pltpu.SMEM((LEAVES,), jnp.int32),
            pltpu.SMEM((1, 4), jnp.int32),
            pltpu.VMEM((NONE + 1, 32, 128), BF),
            pltpu.VMEM((NONE + 1, 32, 128), BF),
            pltpu.VMEM((PER_STEP, 32, 128), F32),
            pltpu.VMEM((LEAVES // GROUP, 128, 256), BF),
            pltpu.VMEM((LEAVES, 4, 128, 128), BF),
            pltpu.VMEM((LEAVES, 4, 1024), BF),
            pltpu.VMEM((1, 4, 1024), BF),
            pltpu.SemaphoreType.DMA((STEPS + 7,)),
        ],
        name="near_far",
        **params(1 << 30),
    )(
        level,
        leaf,
        stays(nearfield_source_leaf.T),
        stays(near_count),
        stays(far_source.T),
        stays(far_count),
        stays(top_source),
        top_count,
        held(packed),
        held(before),
        held(after),
        stays(nearfield_block_matrix),
        stays(far_block),
        stays(top_block),
        held(basis),
    )

    got = {}
    for k, out in ((2, out2), (1, out1), (3, out3)):
        got[k] = lax.ppermute(out, "level", [(n, (n + k) % 4) for n in range(4)])

    result = pl.pallas_call(
        final_kernel,
        out_shape=jax.ShapeDtypeStruct((parts, 16, 128), BF),
        in_specs=[VMEM] * 8,
        out_specs=VMEM,
        scratch_shapes=[
            pltpu.VMEM((4 * ROWS, 128), jnp.int32),
            pltpu.SMEM((4 * ROWS, 128), jnp.int32),
            pltpu.SemaphoreType.DMA,
        ],
        name="final",
        **params(1 << 24),
    )(
        held(roots),
        held(operator),
        held(kept),
        held(top_own),
        held(names_own),
        held(got[1]),
        held(got[2]),
        held(got[3]),
    )
    return result.reshape(LEAVES, ROWS, 128)


def solution(mesh):
    placed = (
        P("leaf", None, None),
        P("leaf", None, None),
        P("leaf", None, None),
        P("leaf", "level"),
        P("leaf"),
        P("leaf", "level", None, None),
        P("leaf", "level"),
        P("leaf"),
        P("leaf", "level", None),
        P("leaf", "level"),
        P("leaf"),
        P("leaf", "level", None),
    )
    return jax.shard_map(
        per_device, mesh=mesh, in_specs=placed, out_specs=P("leaf", "level", None), check_vma=False
    )
```

```python
import jax
import jax.numpy as jnp
from jax import lax
from jax.experimental import pallas as pl
from jax.experimental.pallas import tpu as pltpu
from jax.sharding import PartitionSpec as P

BF = jnp.bfloat16
F32 = jnp.float32
LEAVES = 32
ROOTS = 64
GROUP = 4
PACKED = LEAVES + LEAVES // GROUP
ROWS = 8
STEPS = 2
PER_STEP = LEAVES // STEPS
AHEAD = 2
NONE = 3 * LEAVES


def dot_nt(a, b):
    return lax.dot_general(a, b, (((1,), (1,)), ((), ())), preferred_element_type=F32)


def dot_nn(a, b):
    return lax.dot_general(a, b, (((1,), (0,)), ((), ())), preferred_element_type=F32)


def two_terms(value):
    high = value.astype(BF)
    return high, (value - high.astype(F32)).astype(BF)


def coef_kernel(level, vectors, basis_in, transfer_in, packed, basis, transfer, spread, wide, sems):
    copies = [
        pltpu.make_async_copy(vectors, packed.at[0:LEAVES], sems.at[0]),
        pltpu.make_async_copy(basis_in, basis, sems.at[1]),
        pltpu.make_async_copy(transfer_in, transfer, sems.at[2]),
    ]
    for copy in copies:
        copy.start()
    for copy in copies:
        copy.wait()
    total = jnp.zeros((32, 32), F32)
    for g in range(LEAVES // GROUP):
        pieces = []
        for m in range(GROUP):
            i = g * GROUP + m
            c = dot_nt(packed[i], basis[i]).astype(BF)
            total = total + dot_nt(c, transfer[i])
            pieces.append(c)
        packed[LEAVES + g] = jnp.concatenate(pieces, axis=1)
    wide[...] = jnp.concatenate([total] * GROUP, axis=1)
    root = wide[pl.ds(pl.multiple_of(level[0] * ROWS, ROWS), ROWS), :].astype(BF)
    twice = jnp.concatenate([root, root], axis=0)
    for t in range(ROOTS // 4):
        spread[t] = twice


def couplings(rows4, lane, row):
    x = jnp.concatenate([rows4[:, p * 128 : (p + 1) * 128] for p in range(8)], axis=0)
    out = x
    for d in range(1, 4):
        turned = jnp.where(row < 4 - d, pltpu.roll(x, 32 - d, 0), pltpu.roll(x, 4 - d, 0))
        out = jnp.where((row + d) % 4 == lane, pltpu.roll(turned, 32 * d, 1), out)
    return out


def near_far_kernel(
    level,
    leaf,
    near_source_in,
    near_count_in,
    far_source_in,
    far_count_in,
    top_source_in,
    top_count,
    own,
    inside,
    outside,
    blocks_in,
    far_in,
    top_in,
    basis,
    kept,
    out1,
    out2,
    out3,
    top_own,
    names_own,
    near_source,
    near_count,
    far_source,
    far_count,
    top_source,
    vtab,
    ctab,
    prod,
    terms,
    blocks,
    far,
    top,
    sems,
):
    def stream(n):
        part = pl.ds(n * PER_STEP, PER_STEP)
        return pltpu.make_async_copy(blocks_in.at[part], blocks.at[part], sems.at[n])

    small = [
        pltpu.make_async_copy(a, b, sems.at[STEPS + n])
        for n, (a, b) in enumerate(
            (
                (near_source_in, near_source),
                (near_count_in, near_count),
                (far_source_in, far_source),
                (far_count_in, far_count),
                (top_source_in, top_source),
                (top_in, top),
                (far_in, far),
            )
        )
    ]
    for copy in small:
        copy.start()
    for n in range(AHEAD):
        stream(n).start()
    lane = lax.broadcasted_iota(jnp.int32, (32, 128), 1) // 32
    row = lax.broadcasted_iota(jnp.int32, (32, 128), 0) % 4
    odd = leaf[0] % 2
    for n, part in ((1, own), (2 - 2 * odd, inside), (2 * odd, outside)):
        vtab[pl.ds(n * LEAVES, LEAVES)] = part[0:LEAVES]
        for g in range(LEAVES // GROUP):
            tile = part[LEAVES + g].astype(F32)
            turned = [tile] + [pltpu.roll(tile, 32 * k, 1) for k in range(1, GROUP)]
            for m in range(GROUP):
                v = turned[(0 - m) % GROUP]
                for k in range(1, GROUP):
                    v = jnp.where(lane == k, turned[(k - m) % GROUP], v)
                ctab[n * LEAVES + g * GROUP + m] = v.astype(BF)
    vtab[NONE] = jnp.zeros((32, 128), BF)
    ctab[NONE] = jnp.zeros((32, 128), BF)

    me = level[0]
    first = me * 4
    shift = LEAVES - leaf[0] * LEAVES
    for copy in small:
        copy.wait()
    top_f = couplings(top[0].astype(F32), lane, row).astype(BF)
    top_own[...] = top_f
    row8 = lax.broadcasted_iota(jnp.int32, (16, 128), 0)
    names = jnp.full((16, 128), -1, jnp.int32)
    for s in range(4):
        names = jnp.where(row8 == s, jnp.where(first + s < top_count[0], place(top_source[0, s], leaf[0]), -1), names)
    names_own[...] = names[0:8]
    names = names.astype(F32).astype(BF)
    for out in (out1, out2, out3):
        out[LEAVES // 2] = top_f[0:16]
        out[LEAVES // 2 + 1] = top_f[16:32]
        out[LEAVES // 2 + 2] = names

    same = lax.broadcasted_iota(jnp.int32, (128, 128), 0) // 32 == lax.broadcasted_iota(jnp.int32, (128, 128), 1) // 32
    for g in range(LEAVES // GROUP):
        chosen = []
        matrices = []
        for m in range(GROUP):
            i = g * GROUP + m
            far_at = [jnp.where(first + s < far_count[i], far_source[s, i] + shift, NONE) for s in range(4)]
            c = ctab[far_at[0]]
            for s in range(1, 4):
                c = jnp.where(lane == s, ctab[far_at[s]], c)
            chosen.append(c)
            matrices.append(couplings(far[i].astype(F32), lane, row).astype(BF))
        down = dot_nt(jnp.concatenate(chosen, axis=0), jnp.concatenate(matrices, axis=0))
        terms[g] = jnp.concatenate(two_terms(jnp.where(same, down, 0.0)), axis=1)

    @pl.loop(0, STEPS)
    def _(step):
        stream(step).wait()

        @pl.when(step + AHEAD < STEPS)
        def _():
            stream(step + AHEAD).start()

        for h in range(PER_STEP // GROUP):
            g = step * (PER_STEP // GROUP) + h
            b = basis[pl.ds(g * GROUP, GROUP)].reshape(GROUP * 32, 128)
            value = dot_nn(terms[g], jnp.concatenate([b, b], axis=0))
            for m in range(GROUP):
                i = g * GROUP + m
                near_at = [jnp.where(first + s < near_count[i], near_source[s, i] + shift, NONE) for s in range(4)]
                total = value[m * 32 : m * 32 + 32]
                for s in range(0, 4, 2):
                    lhs = jnp.concatenate([vtab[near_at[s]], vtab[near_at[s + 1]]], axis=1)
                    rhs = jnp.concatenate([blocks[i, s], blocks[i, s + 1]], axis=1)
                    total = total + dot_nt(lhs, rhs)
                prod[h * GROUP + m] = total
            for m in range(0, GROUP, 2):
                pair = (step * PER_STEP + h * GROUP + m) // 2

                def rows(k):
                    at = pl.multiple_of((me ^ k) * ROWS, ROWS)
                    n = h * GROUP + m
                    return jnp.concatenate([prod[n, pl.ds(at, ROWS), :], prod[n + 1, pl.ds(at, ROWS), :]], axis=0)

                kept[pair] = rows(0)
                for k, out in ((1, out1), (2, out2), (3, out3)):
                    out[pair] = rows(k).astype(BF)


def top_operator_kernel(transfer, basis, operator):
    for i in range(LEAVES):
        high, low = two_terms(dot_nn(transfer[i], basis[i]))
        operator[0:32, i * 128 : (i + 1) * 128] = high
        operator[32:64, i * 128 : (i + 1) * 128] = low


def final_kernel(roots, other_roots, operator, kept, top_own, names_own, got2, got1, got3, out):
    others = (got1, got2, got3)
    tiles = [names_own[...].astype(F32)]
    for got in others:
        tiles.append(got[LEAVES // 2 + 2].astype(F32)[0:ROWS])
    for h in range(LEAVES // 2):
        kept[h] = kept[h] + got1[h].astype(F32) + got2[h].astype(F32) + got3[h].astype(F32)
    lane = lax.broadcasted_iota(jnp.int32, (ROWS, 128), 1) // 32
    total = jnp.zeros((ROWS, 32), F32)
    for k in range(4):
        c = jnp.zeros((ROWS, 128), F32)
        for s in range(4):
            at = jnp.max(tiles[k][s : s + 1]).astype(jnp.int32)
            spot = jnp.maximum(at, 0)
            index = spot % (ROOTS // 2)
            tile = jnp.where(spot < ROOTS // 2, roots[index].astype(F32), other_roots[index].astype(F32))
            c = jnp.where((lane == s) & (at >= 0), tile, c)
        c = c.astype(BF)
        if k == 0:
            total = total + dot_nt(c, top_own[...])
        else:
            got = others[k - 1]
            total = total + dot_nt(c, jnp.concatenate([got[LEAVES // 2], got[LEAVES // 2 + 1]], axis=0))
    high, low = two_terms(total)
    lhs = jnp.concatenate([high, low, high], axis=1)
    for h in range(LEAVES // 2):
        w = operator[:, h * 256 : (h + 1) * 256]
        t = dot_nn(lhs, jnp.concatenate([w[0:32], w[0:32], w[32:64]], axis=0))
        out[h] = (kept[h] + jnp.concatenate([t[:, 0:128], t[:, 128:256]], axis=0)).astype(BF)


SMEM = pl.BlockSpec(memory_space=pltpu.SMEM)
VMEM = pl.BlockSpec(memory_space=pltpu.VMEM)
HBM = pl.BlockSpec(memory_space=pltpu.HBM)
LIMIT = 16 * 1024 * 1024


def held(value):
    return pltpu.with_memory_space_constraint(value, pltpu.VMEM)


def stays(value):
    return pltpu.with_memory_space_constraint(value, pltpu.HBM)


def params(flops):
    return dict(
        compiler_params=pltpu.CompilerParams(vmem_limit_bytes=LIMIT),
        cost_estimate=pl.CostEstimate(flops=flops, bytes_accessed=1 << 20, transcendentals=0),
    )


def gathered(spread):
    halves = [[n for n in range(ROOTS) if n // 4 % 2 == h] for h in range(2)]
    return lax.all_to_all(spread, "leaf", 0, 0, tiled=True, axis_index_groups=halves)


def place(source, leaf):
    return ((source ^ leaf) // 4 % 2) * (ROOTS // 2) + source // 8 * 4 + source % 4


def per_device(
    vectors,
    leaf_basis,
    transfer,
    nearfield_source_leaf,
    near_count,
    nearfield_block_matrix,
    far_source,
    far_count,
    far_block,
    top_source,
    top_count,
    top_block,
):
    level = lax.axis_index("level").astype(jnp.int32).reshape(1)
    leaf = lax.axis_index("leaf").astype(jnp.int32).reshape(1)
    packed, basis, carried, spread = pl.pallas_call(
        coef_kernel,
        out_shape=(
            pltpu.VMEM((PACKED, 32, 128), BF),
            pltpu.VMEM((LEAVES, 32, 128), BF),
            pltpu.VMEM((LEAVES, 32, 32), BF),
            pltpu.VMEM((ROOTS // 4, 2 * ROWS, 128), BF),
        ),
        in_specs=[SMEM] + [HBM] * 3,
        out_specs=(VMEM,) * 4,
        scratch_shapes=[pltpu.VMEM((32, 128), F32), pltpu.SemaphoreType.DMA((3,))],
        name="coefficients",
        **params(1 << 24),
    )(level, stays(vectors), stays(leaf_basis), stays(transfer))

    inside = lax.ppermute(packed, "leaf", [(n, n ^ 1) for n in range(64)])
    outside = lax.ppermute(packed, "leaf", [(n, ((n + 1) ^ 1) - 1) for n in range(1, 63)])
    roots = gathered(spread.reshape(ROOTS // 2, ROWS, 128))

    operator = pl.pallas_call(
        top_operator_kernel,
        out_shape=pltpu.VMEM((64, LEAVES * 128), BF),
        in_specs=[VMEM, VMEM],
        out_specs=VMEM,
        name="top_operator",
        **params(1 << 24),
    )(held(carried), held(basis))

    parts = LEAVES // 2
    sent = pltpu.VMEM((parts + 3, 16, 128), BF)
    kept, out1, out2, out3, top_own, names_own = pl.pallas_call(
        near_far_kernel,
        out_shape=(
            pltpu.VMEM((parts, 16, 128), F32),
            sent,
            sent,
            sent,
            pltpu.VMEM((32, 128), BF),
            pltpu.VMEM((ROWS, 128), jnp.int32),
        ),
        in_specs=[SMEM] * 2 + [HBM] * 5 + [SMEM] + [VMEM] * 3 + [HBM] * 3 + [VMEM],
        out_specs=(VMEM,) * 6,
        scratch_shapes=[
            pltpu.SMEM((4, LEAVES), jnp.int32),
            pltpu.SMEM((LEAVES,), jnp.int32),
            pltpu.SMEM((4, LEAVES), jnp.int32),
            pltpu.SMEM((LEAVES,), jnp.int32),
            pltpu.SMEM((1, 4), jnp.int32),
            pltpu.VMEM((NONE + 1, 32, 128), BF),
            pltpu.VMEM((NONE + 1, 32, 128), BF),
            pltpu.VMEM((PER_STEP, 32, 128), F32),
            pltpu.VMEM((LEAVES // GROUP, 128, 256), BF),
            pltpu.VMEM((LEAVES, 4, 128, 128), BF),
            pltpu.VMEM((LEAVES, 4, 1024), BF),
            pltpu.VMEM((1, 4, 1024), BF),
            pltpu.SemaphoreType.DMA((STEPS + 7,)),
        ],
        name="near_far",
        **params(1 << 30),
    )(
        level,
        leaf,
        stays(nearfield_source_leaf.T),
        stays(near_count),
        stays(far_source.T),
        stays(far_count),
        stays(top_source),
        top_count,
        held(packed),
        held(inside),
        held(outside),
        stays(nearfield_block_matrix),
        stays(far_block),
        stays(top_block),
        held(basis),
    )

    got = {}
    for k, out in ((2, out2), (1, out1), (3, out3)):
        got[k] = lax.ppermute(out, "level", [(n, n ^ k) for n in range(4)])

    other_roots = lax.ppermute(roots, "leaf", [(n, n ^ 6) for n in range(ROOTS)])

    result = pl.pallas_call(
        final_kernel,
        out_shape=jax.ShapeDtypeStruct((parts, 16, 128), BF),
        in_specs=[VMEM] * 9,
        out_specs=VMEM,
        name="final",
        **params(1 << 24),
    )(
        held(roots),
        held(other_roots),
        held(operator),
        held(kept),
        held(top_own),
        held(names_own),
        held(got[2]),
        held(got[1]),
        held(got[3]),
    )
    return result.reshape(LEAVES, ROWS, 128)


def solution(mesh):
    placed = (
        P("leaf", None, None),
        P("leaf", None, None),
        P("leaf", None, None),
        P("leaf", "level"),
        P("leaf"),
        P("leaf", "level", None, None),
        P("leaf", "level"),
        P("leaf"),
        P("leaf", "level", None),
        P("leaf", "level"),
        P("leaf"),
        P("leaf", "level", None),
    )
    return jax.shard_map(
        per_device, mesh=mesh, in_specs=placed, out_specs=P("leaf", "level", None), check_vma=False
    )
```

```python
import jax
import jax.numpy as jnp
from jax import lax
from jax.experimental import pallas as pl
from jax.experimental.pallas import tpu as pltpu
from jax.sharding import PartitionSpec as P

BF = jnp.bfloat16
F32 = jnp.float32
LEAVES = 32
ROOTS = 64
GROUP = 4
PACKED = LEAVES + LEAVES // GROUP
ROWS = 8
STEPS = 2
PER_STEP = LEAVES // STEPS
AHEAD = 2
NONE = 3 * LEAVES


def dot_nt(a, b):
    return lax.dot_general(a, b, (((1,), (1,)), ((), ())), preferred_element_type=F32)


def dot_nn(a, b):
    return lax.dot_general(a, b, (((1,), (0,)), ((), ())), preferred_element_type=F32)


def two_terms(value):
    high = value.astype(BF)
    return high, (value - high.astype(F32)).astype(BF)


def coef_kernel(
    vectors,
    basis_in,
    transfer_in,
    far_in,
    top_in,
    near_source_in,
    near_count_in,
    far_source_in,
    far_count_in,
    top_source_in,
    packed,
    basis,
    transfer,
    root_out,
    far,
    top,
    near_source,
    near_count,
    far_source,
    far_count,
    top_source,
    wide,
    sems,
):
    pairs = (
        (vectors, packed.at[0:LEAVES]),
        (basis_in, basis),
        (transfer_in, transfer),
        (far_in, far),
        (near_source_in, near_source),
        (near_count_in, near_count),
        (far_source_in, far_source),
        (far_count_in, far_count),
        (top_in, top),
        (top_source_in, top_source),
    )
    copies = [pltpu.make_async_copy(a, b, sems.at[n]) for n, (a, b) in enumerate(pairs)]
    for copy in copies:
        copy.start()
    for copy in copies[:3]:
        copy.wait()
    total = jnp.zeros((32, 32), F32)
    for g in range(LEAVES // GROUP):
        pieces = []
        for m in range(GROUP):
            i = g * GROUP + m
            c = dot_nt(packed[i], basis[i]).astype(BF)
            total = total + dot_nt(c, transfer[i])
            pieces.append(c)
        packed[LEAVES + g] = jnp.concatenate(pieces, axis=1)
    wide[...] = jnp.concatenate([total] * GROUP, axis=1)
    root = wide[pl.ds(pl.multiple_of(lax.axis_index("level") * ROWS, ROWS), ROWS), :].astype(BF)
    root_out[...] = jnp.concatenate([root, root], axis=0)
    for copy in copies[3:]:
        copy.wait()


def spread_kernel(root, spread):
    for t in range(ROOTS // 4):
        spread[t] = root[...]


def couplings(rows4, lane, row):
    x = jnp.concatenate([rows4[:, p * 128 : (p + 1) * 128] for p in range(8)], axis=0)
    out = x
    for d in range(1, 4):
        turned = jnp.where(row < 4 - d, pltpu.roll(x, 32 - d, 0), pltpu.roll(x, 4 - d, 0))
        out = jnp.where((row + d) % 4 == lane, pltpu.roll(turned, 32 * d, 1), out)
    return out


def near_far_kernel(
    near_source_in,
    near_count_in,
    far_source_in,
    far_count_in,
    top_source_in,
    own,
    outside,
    inside,
    blocks_in,
    far,
    top,
    basis,
    kept,
    out1,
    out2,
    out3,
    top_own,
    names_own,
    near_source,
    near_count,
    far_source,
    far_count,
    top_source,
    vtab,
    ctab,
    prod,
    terms,
    blocks,
    sems,
):
    def stream(n):
        part = pl.ds(n * PER_STEP, PER_STEP)
        return pltpu.make_async_copy(blocks_in.at[part], blocks.at[part], sems.at[n])

    small = [
        pltpu.make_async_copy(a, b, sems.at[STEPS + n])
        for n, (a, b) in enumerate(
            (
                (near_source_in, near_source),
                (near_count_in, near_count),
                (far_source_in, far_source),
                (far_count_in, far_count),
                (top_source_in, top_source),
            )
        )
    ]
    for copy in small:
        copy.start()
    for n in range(AHEAD):
        stream(n).start()
    lane = lax.broadcasted_iota(jnp.int32, (32, 128), 1) // 32
    row = lax.broadcasted_iota(jnp.int32, (32, 128), 0) % 4
    me = lax.axis_index("level")
    leaf = lax.axis_index("leaf")
    first = me * 4
    odd = leaf % 2
    for n, part in ((1, own), (2 - 2 * odd, inside), (2 * odd, outside)):
        vtab[pl.ds(n * LEAVES, LEAVES)] = part[0:LEAVES]
        for g in range(LEAVES // GROUP):
            tile = part[LEAVES + g].astype(F32)
            turned = [tile] + [pltpu.roll(tile, 32 * k, 1) for k in range(1, GROUP)]
            for m in range(GROUP):
                v = turned[(0 - m) % GROUP]
                for k in range(1, GROUP):
                    v = jnp.where(lane == k, turned[(k - m) % GROUP], v)
                ctab[n * LEAVES + g * GROUP + m] = v.astype(BF)
    vtab[NONE] = jnp.zeros((32, 128), BF)
    ctab[NONE] = jnp.zeros((32, 128), BF)

    shift = LEAVES - leaf * LEAVES
    for copy in small:
        copy.wait()
    top_f = couplings(top[0].astype(F32), lane, row).astype(BF)
    top_own[...] = top_f
    row8 = lax.broadcasted_iota(jnp.int32, (16, 128), 0)
    names = jnp.zeros((16, 128), jnp.int32)
    for s in range(4):
        names = jnp.where(row8 == s, place(top_source[0, s], leaf), names)
    names_own[...] = names[0:8]
    names = names.astype(F32).astype(BF)
    for out in (out1, out2, out3):
        out[LEAVES // 2] = top_f[0:16]
        out[LEAVES // 2 + 1] = top_f[16:32]
        out[LEAVES // 2 + 2] = names

    same = lax.broadcasted_iota(jnp.int32, (128, 128), 0) // 32 == lax.broadcasted_iota(jnp.int32, (128, 128), 1) // 32
    for g in range(LEAVES // GROUP):
        chosen = []
        matrices = []
        for m in range(GROUP):
            i = g * GROUP + m
            far_at = [jnp.where(first + s < far_count[i], far_source[s, i] + shift, NONE) for s in range(4)]
            c = ctab[far_at[0]]
            for s in range(1, 4):
                c = jnp.where(lane == s, ctab[far_at[s]], c)
            chosen.append(c)
            matrices.append(couplings(far[i].astype(F32), lane, row).astype(BF))
        down = dot_nt(jnp.concatenate(chosen, axis=0), jnp.concatenate(matrices, axis=0))
        terms[g] = jnp.concatenate(two_terms(jnp.where(same, down, 0.0)), axis=1)

    @pl.loop(0, STEPS)
    def _(step):
        stream(step).wait()

        @pl.when(step + AHEAD < STEPS)
        def _():
            stream(step + AHEAD).start()

        for h in range(PER_STEP // GROUP):
            g = step * (PER_STEP // GROUP) + h
            b = basis[pl.ds(g * GROUP, GROUP)].reshape(GROUP * 32, 128)
            value = dot_nn(terms[g], jnp.concatenate([b, b], axis=0))
            for m in range(GROUP):
                i = g * GROUP + m
                near_at = [jnp.where(first + s < near_count[i], near_source[s, i] + shift, NONE) for s in range(4)]
                total = value[m * 32 : m * 32 + 32]
                for s in range(0, 4, 2):
                    lhs = jnp.concatenate([vtab[near_at[s]], vtab[near_at[s + 1]]], axis=1)
                    rhs = jnp.concatenate([blocks[i, s], blocks[i, s + 1]], axis=1)
                    total = total + dot_nt(lhs, rhs)
                prod[h * GROUP + m] = total
            for m in range(0, GROUP, 2):
                pair = (step * PER_STEP + h * GROUP + m) // 2

                def rows(k):
                    at = pl.multiple_of((me ^ k) * ROWS, ROWS)
                    n = h * GROUP + m
                    return jnp.concatenate([prod[n, pl.ds(at, ROWS), :], prod[n + 1, pl.ds(at, ROWS), :]], axis=0)

                kept[pair] = rows(0)
                for k, out in ((1, out1), (2, out2), (3, out3)):
                    out[pair] = rows(k).astype(BF)


def top_operator_kernel(transfer, basis, operator):
    for i in range(LEAVES):
        high, low = two_terms(dot_nn(transfer[i], basis[i]))
        operator[0:32, i * 128 : (i + 1) * 128] = high
        operator[32:64, i * 128 : (i + 1) * 128] = low


def final_kernel(top_count, roots, other_roots, operator, kept, top_own, names_own, got2, got1, got3, out):
    others = (got1, got2, got3)
    me = lax.axis_index("level")
    tiles = [names_own[...].astype(F32)]
    for got in others:
        tiles.append(got[LEAVES // 2 + 2].astype(F32)[0:ROWS])
    for h in range(LEAVES // 2):
        kept[h] = kept[h] + got1[h].astype(F32) + got2[h].astype(F32) + got3[h].astype(F32)
    lane = lax.broadcasted_iota(jnp.int32, (ROWS, 128), 1) // 32
    total = jnp.zeros((ROWS, 32), F32)
    for k in range(4):
        c = jnp.zeros((ROWS, 128), F32)
        for s in range(4):
            spot = jnp.max(tiles[k][s : s + 1]).astype(jnp.int32)
            index = spot % (ROOTS // 2)
            tile = jnp.where(spot < ROOTS // 2, roots[index].astype(F32), other_roots[index].astype(F32))
            live = (me ^ k) * 4 + s < top_count[0]
            c = jnp.where((lane == s) & live, tile, c)
        c = c.astype(BF)
        if k == 0:
            total = total + dot_nt(c, top_own[...])
        else:
            got = others[k - 1]
            total = total + dot_nt(c, jnp.concatenate([got[LEAVES // 2], got[LEAVES // 2 + 1]], axis=0))
    high, low = two_terms(total)
    lhs = jnp.concatenate([high, low, high], axis=1)
    for h in range(LEAVES // 2):
        w = operator[:, h * 256 : (h + 1) * 256]
        t = dot_nn(lhs, jnp.concatenate([w[0:32], w[0:32], w[32:64]], axis=0))
        out[h] = (kept[h] + jnp.concatenate([t[:, 0:128], t[:, 128:256]], axis=0)).astype(BF)


SMEM = pl.BlockSpec(memory_space=pltpu.SMEM)
VMEM = pl.BlockSpec(memory_space=pltpu.VMEM)
HBM = pl.BlockSpec(memory_space=pltpu.HBM)
LIMIT = 16 * 1024 * 1024


def held(value):
    return pltpu.with_memory_space_constraint(value, pltpu.VMEM)


def stays(value):
    return pltpu.with_memory_space_constraint(value, pltpu.HBM)


def params(flops):
    return dict(
        compiler_params=pltpu.CompilerParams(vmem_limit_bytes=LIMIT),
        cost_estimate=pl.CostEstimate(flops=flops, bytes_accessed=1 << 20, transcendentals=0),
    )


def gathered(spread):
    halves = [[n for n in range(ROOTS) if n // 4 % 2 == h] for h in range(2)]
    return lax.all_to_all(spread, "leaf", 0, 0, tiled=True, axis_index_groups=halves)


def place(source, leaf):
    return ((source ^ leaf) // 4 % 2) * (ROOTS // 2) + source // 8 * 4 + source % 4


def per_device(
    vectors,
    leaf_basis,
    transfer,
    nearfield_source_leaf,
    near_count,
    nearfield_block_matrix,
    far_source,
    far_count,
    far_block,
    top_source,
    top_count,
    top_block,
):
    packed, basis, carried, root, far, top, near_at, near_n, far_at, far_n, top_at = pl.pallas_call(
        coef_kernel,
        out_shape=(
            pltpu.VMEM((PACKED, 32, 128), BF),
            pltpu.VMEM((LEAVES, 32, 128), BF),
            pltpu.VMEM((LEAVES, 32, 32), BF),
            pltpu.VMEM((2 * ROWS, 128), BF),
            pltpu.VMEM((LEAVES, 4, 1024), BF),
            pltpu.VMEM((1, 4, 1024), BF),
            pltpu.VMEM((4, LEAVES), jnp.int32),
            pltpu.VMEM((LEAVES,), jnp.int32),
            pltpu.VMEM((4, LEAVES), jnp.int32),
            pltpu.VMEM((LEAVES,), jnp.int32),
            pltpu.VMEM((1, 4), jnp.int32),
        ),
        in_specs=[HBM] * 10,
        out_specs=(VMEM,) * 11,
        scratch_shapes=[pltpu.VMEM((32, 128), F32), pltpu.SemaphoreType.DMA((10,))],
        name="coefficients",
        **params(1 << 24),
    )(
        stays(vectors),
        stays(leaf_basis),
        stays(transfer),
        stays(far_block),
        stays(top_block),
        stays(nearfield_source_leaf.T),
        stays(near_count),
        stays(far_source.T),
        stays(far_count),
        stays(top_source),
    )

    outside = lax.ppermute(packed, "leaf", [(n, ((n + 1) ^ 1) - 1) for n in range(1, 63)])
    inside = lax.ppermute(packed, "leaf", [(n, n ^ 1) for n in range(64)])
    spread = pl.pallas_call(
        spread_kernel,
        out_shape=jax.ShapeDtypeStruct((ROOTS // 4, 2 * ROWS, 128), BF),
        in_specs=[VMEM],
        out_specs=VMEM,
        name="spread",
        **params(1 << 20),
    )(held(root))
    roots = gathered(spread.reshape(ROOTS // 2, ROWS, 128))

    operator = pl.pallas_call(
        top_operator_kernel,
        out_shape=pltpu.VMEM((64, LEAVES * 128), BF),
        in_specs=[VMEM, VMEM],
        out_specs=VMEM,
        name="top_operator",
        **params(1 << 24),
    )(held(carried), held(basis))

    parts = LEAVES // 2
    sent = pltpu.VMEM((parts + 3, 16, 128), BF)
    kept, out1, out2, out3, top_own, names_own = pl.pallas_call(
        near_far_kernel,
        out_shape=(
            pltpu.VMEM((parts, 16, 128), F32),
            sent,
            sent,
            sent,
            pltpu.VMEM((32, 128), BF),
            pltpu.VMEM((ROWS, 128), jnp.int32),
        ),
        in_specs=[VMEM] * 8 + [HBM] + [VMEM] * 3,
        out_specs=(VMEM,) * 6,
        scratch_shapes=[
            pltpu.SMEM((4, LEAVES), jnp.int32),
            pltpu.SMEM((LEAVES,), jnp.int32),
            pltpu.SMEM((4, LEAVES), jnp.int32),
            pltpu.SMEM((LEAVES,), jnp.int32),
            pltpu.SMEM((1, 4), jnp.int32),
            pltpu.VMEM((NONE + 1, 32, 128), BF),
            pltpu.VMEM((NONE + 1, 32, 128), BF),
            pltpu.VMEM((PER_STEP, 32, 128), F32),
            pltpu.VMEM((LEAVES // GROUP, 128, 256), BF),
            pltpu.VMEM((LEAVES, 4, 128, 128), BF),
            pltpu.SemaphoreType.DMA((STEPS + 5,)),
        ],
        name="near_far",
        **params(1 << 30),
    )(
        held(near_at),
        held(near_n),
        held(far_at),
        held(far_n),
        held(top_at),
        held(packed),
        held(outside),
        held(inside),
        stays(nearfield_block_matrix),
        held(far),
        held(top),
        held(basis),
    )

    got = {}
    for k, out in ((2, out2), (1, out1), (3, out3)):
        got[k] = lax.ppermute(out, "level", [(n, n ^ k) for n in range(4)])

    other_roots = lax.ppermute(roots, "leaf", [(n, n ^ 6) for n in range(ROOTS)])

    result = pl.pallas_call(
        final_kernel,
        out_shape=jax.ShapeDtypeStruct((parts, 16, 128), BF),
        in_specs=[SMEM] + [VMEM] * 9,
        out_specs=VMEM,
        name="final",
        **params(1 << 24),
    )(
        top_count,
        held(roots),
        held(other_roots),
        held(operator),
        held(kept),
        held(top_own),
        held(names_own),
        held(got[2]),
        held(got[1]),
        held(got[3]),
    )
    return result.reshape(LEAVES, ROWS, 128)


def solution(mesh):
    placed = (
        P("leaf", None, None),
        P("leaf", None, None),
        P("leaf", None, None),
        P("leaf", "level"),
        P("leaf"),
        P("leaf", "level", None, None),
        P("leaf", "level"),
        P("leaf"),
        P("leaf", "level", None),
        P("leaf", "level"),
        P("leaf"),
        P("leaf", "level", None),
    )
    return jax.shard_map(
        per_device, mesh=mesh, in_specs=placed, out_specs=P("leaf", "level", None), check_vma=False
    )
```

```python
import jax
import jax.numpy as jnp
from jax import lax
from jax.experimental import pallas as pl
from jax.experimental.pallas import tpu as pltpu
from jax.sharding import PartitionSpec as P

BF = jnp.bfloat16
F32 = jnp.float32
LEAVES = 32
ROOTS = 64
GROUP = 4
PACKED = LEAVES + LEAVES // GROUP
ROWS = 8
STEPS = 2
PER_STEP = LEAVES // STEPS
AHEAD = 2
NONE = 3 * LEAVES


def dot_nt(a, b):
    return lax.dot_general(a, b, (((1,), (1,)), ((), ())), preferred_element_type=F32)


def dot_nn(a, b):
    return lax.dot_general(a, b, (((1,), (0,)), ((), ())), preferred_element_type=F32)


def two_terms(value):
    high = value.astype(BF)
    return high, (value - high.astype(F32)).astype(BF)


def coef_kernel(
    vectors,
    basis_in,
    transfer_in,
    far_in,
    top_in,
    near_source_in,
    near_count_in,
    far_source_in,
    far_count_in,
    top_source_in,
    packed,
    basis,
    transfer,
    root_out,
    far,
    top,
    near_source,
    near_count,
    far_source,
    far_count,
    top_source,
    wide,
    sems,
):
    pairs = (
        (vectors, packed.at[0:LEAVES]),
        (basis_in, basis),
        (transfer_in, transfer),
        (far_in, far),
        (near_source_in, near_source),
        (near_count_in, near_count),
        (far_source_in, far_source),
        (far_count_in, far_count),
        (top_in, top),
        (top_source_in, top_source),
    )
    copies = [pltpu.make_async_copy(a, b, sems.at[n]) for n, (a, b) in enumerate(pairs)]
    for copy in copies:
        copy.start()
    for copy in copies[:3]:
        copy.wait()
    total = jnp.zeros((32, 32), F32)
    for g in range(LEAVES // GROUP):
        pieces = []
        for m in range(GROUP):
            i = g * GROUP + m
            c = dot_nt(packed[i], basis[i]).astype(BF)
            total = total + dot_nt(c, transfer[i])
            pieces.append(c)
        packed[LEAVES + g] = jnp.concatenate(pieces, axis=1)
    wide[...] = jnp.concatenate([total] * GROUP, axis=1)
    root = wide[pl.ds(pl.multiple_of(lax.axis_index("level") * ROWS, ROWS), ROWS), :].astype(BF)
    root_out[...] = jnp.concatenate([root, root], axis=0)
    for copy in copies[3:]:
        copy.wait()


def spread_kernel(root, spread):
    for t in range(ROOTS // 4):
        spread[t] = root[...]


def couplings(rows4, lane, row):
    x = jnp.concatenate([rows4[:, p * 128 : (p + 1) * 128] for p in range(8)], axis=0)
    out = x
    for d in range(1, 4):
        turned = jnp.where(row < 4 - d, pltpu.roll(x, 32 - d, 0), pltpu.roll(x, 4 - d, 0))
        out = jnp.where((row + d) % 4 == lane, pltpu.roll(turned, 32 * d, 1), out)
    return out


def near_far_kernel(
    near_source_in,
    near_count_in,
    far_source_in,
    far_count_in,
    top_source_in,
    own,
    outside,
    inside,
    blocks_in,
    far,
    top,
    basis,
    kept,
    out1,
    out2,
    out3,
    top_own,
    names_own,
    near_source,
    near_count,
    far_source,
    far_count,
    top_source,
    vtab,
    ctab,
    prod,
    terms,
    blocks,
    sems,
):
    def stream(n):
        part = pl.ds(n * PER_STEP, PER_STEP)
        return pltpu.make_async_copy(blocks_in.at[part], blocks.at[part], sems.at[n])

    small = [
        pltpu.make_async_copy(a, b, sems.at[STEPS + n])
        for n, (a, b) in enumerate(
            (
                (near_source_in, near_source),
                (near_count_in, near_count),
                (far_source_in, far_source),
                (far_count_in, far_count),
                (top_source_in, top_source),
            )
        )
    ]
    for copy in small:
        copy.start()
    for n in range(AHEAD):
        stream(n).start()
    lane = lax.broadcasted_iota(jnp.int32, (32, 128), 1) // 32
    row = lax.broadcasted_iota(jnp.int32, (32, 128), 0) % 4
    me = lax.axis_index("level")
    leaf = lax.axis_index("leaf")
    first = me * 4
    odd = leaf % 2
    for n, part in ((1, own), (2 - 2 * odd, inside), (2 * odd, outside)):
        vtab[pl.ds(n * LEAVES, LEAVES)] = part[0:LEAVES]
        for g in range(LEAVES // GROUP):
            tile = part[LEAVES + g].astype(F32)
            turned = [tile] + [pltpu.roll(tile, 32 * k, 1) for k in range(1, GROUP)]
            for m in range(GROUP):
                v = turned[(0 - m) % GROUP]
                for k in range(1, GROUP):
                    v = jnp.where(lane == k, turned[(k - m) % GROUP], v)
                ctab[n * LEAVES + g * GROUP + m] = v.astype(BF)
    vtab[NONE] = jnp.zeros((32, 128), BF)
    ctab[NONE] = jnp.zeros((32, 128), BF)

    shift = LEAVES - leaf * LEAVES
    for copy in small:
        copy.wait()
    top_f = couplings(top[0].astype(F32), lane, row).astype(BF)
    top_own[...] = top_f
    row8 = lax.broadcasted_iota(jnp.int32, (16, 128), 0)
    names = jnp.zeros((16, 128), jnp.int32)
    for s in range(4):
        names = jnp.where(row8 == s, place(top_source[0, s], leaf), names)
    names_own[...] = names[0:8]
    names = names.astype(F32).astype(BF)
    for out in (out1, out2, out3):
        out[LEAVES // 2] = top_f[0:16]
        out[LEAVES // 2 + 1] = top_f[16:32]
        out[LEAVES // 2 + 2] = names

    same = lax.broadcasted_iota(jnp.int32, (128, 128), 0) // 32 == lax.broadcasted_iota(jnp.int32, (128, 128), 1) // 32
    for g in range(LEAVES // GROUP):
        chosen = []
        matrices = []
        for m in range(GROUP):
            i = g * GROUP + m
            far_at = [jnp.where(first + s < far_count[i], far_source[s, i] + shift, NONE) for s in range(4)]
            c = ctab[far_at[0]]
            for s in range(1, 4):
                c = jnp.where(lane == s, ctab[far_at[s]], c)
            chosen.append(c)
            matrices.append(couplings(far[i].astype(F32), lane, row).astype(BF))
        down = dot_nt(jnp.concatenate(chosen, axis=0), jnp.concatenate(matrices, axis=0))
        terms[g] = jnp.concatenate(two_terms(jnp.where(same, down, 0.0)), axis=1)

    @pl.loop(0, STEPS)
    def _(step):
        stream(step).wait()

        @pl.when(step + AHEAD < STEPS)
        def _():
            stream(step + AHEAD).start()

        for h in range(PER_STEP // GROUP):
            g = step * (PER_STEP // GROUP) + h
            b = basis[pl.ds(g * GROUP, GROUP)].reshape(GROUP * 32, 128)
            value = dot_nn(terms[g], jnp.concatenate([b, b], axis=0))
            for m in range(GROUP):
                i = g * GROUP + m
                near_at = [jnp.where(first + s < near_count[i], near_source[s, i] + shift, NONE) for s in range(4)]
                total = value[m * 32 : m * 32 + 32]
                for s in range(0, 4, 2):
                    lhs = jnp.concatenate([vtab[near_at[s]], vtab[near_at[s + 1]]], axis=1)
                    rhs = jnp.concatenate([blocks[i, s], blocks[i, s + 1]], axis=1)
                    total = total + dot_nt(lhs, rhs)
                prod[h * GROUP + m] = total
            for m in range(0, GROUP, 2):
                pair = (step * PER_STEP + h * GROUP + m) // 2

                def rows(k):
                    at = pl.multiple_of((me ^ k) * ROWS, ROWS)
                    n = h * GROUP + m
                    return jnp.concatenate([prod[n, pl.ds(at, ROWS), :], prod[n + 1, pl.ds(at, ROWS), :]], axis=0)

                kept[pair] = rows(0)
                for k, out in ((1, out1), (2, out2), (3, out3)):
                    out[pair] = rows(k).astype(BF)


def top_operator_kernel(transfer, basis, operator):
    for i in range(LEAVES):
        high, low = two_terms(dot_nn(transfer[i], basis[i]))
        operator[0:32, i * 128 : (i + 1) * 128] = high
        operator[32:64, i * 128 : (i + 1) * 128] = low


def final_kernel(top_count, roots, other_roots, operator, kept, top_own, names_own, got2, got1, got3, out):
    others = (got1, got2, got3)
    me = lax.axis_index("level")
    tiles = [names_own[...].astype(F32)]
    for got in others:
        tiles.append(got[LEAVES // 2 + 2].astype(F32)[0:ROWS])
    for h in range(LEAVES // 2):
        kept[h] = kept[h] + got1[h].astype(F32) + got2[h].astype(F32) + got3[h].astype(F32)
    lane = lax.broadcasted_iota(jnp.int32, (ROWS, 128), 1) // 32
    total = jnp.zeros((ROWS, 32), F32)
    for k in range(4):
        c = jnp.zeros((ROWS, 128), F32)
        for s in range(4):
            spot = jnp.max(tiles[k][s : s + 1]).astype(jnp.int32)
            index = spot % (ROOTS // 2)
            tile = jnp.where(spot < ROOTS // 2, roots[index].astype(F32), other_roots[index].astype(F32))
            live = (me ^ k) * 4 + s < top_count[0]
            c = jnp.where((lane == s) & live, tile, c)
        c = c.astype(BF)
        if k == 0:
            total = total + dot_nt(c, top_own[...])
        else:
            got = others[k - 1]
            total = total + dot_nt(c, jnp.concatenate([got[LEAVES // 2], got[LEAVES // 2 + 1]], axis=0))
    high, low = two_terms(total)
    lhs = jnp.concatenate([high, low, high], axis=1)
    for h in range(LEAVES // 2):
        w = operator[:, h * 256 : (h + 1) * 256]
        t = dot_nn(lhs, jnp.concatenate([w[0:32], w[0:32], w[32:64]], axis=0))
        out[h] = (kept[h] + jnp.concatenate([t[:, 0:128], t[:, 128:256]], axis=0)).astype(BF)


SMEM = pl.BlockSpec(memory_space=pltpu.SMEM)
VMEM = pl.BlockSpec(memory_space=pltpu.VMEM)
HBM = pl.BlockSpec(memory_space=pltpu.HBM)
LIMIT = 16 * 1024 * 1024


def held(value):
    return pltpu.with_memory_space_constraint(value, pltpu.VMEM)


def stays(value):
    return pltpu.with_memory_space_constraint(value, pltpu.HBM)


def params(flops):
    return dict(
        compiler_params=pltpu.CompilerParams(vmem_limit_bytes=LIMIT),
        cost_estimate=pl.CostEstimate(flops=flops, bytes_accessed=1 << 20, transcendentals=0),
    )


def gathered(spread):
    halves = [[n for n in range(ROOTS) if n // 4 % 2 == h] for h in range(2)]
    return lax.all_to_all(spread, "leaf", 0, 0, tiled=True, axis_index_groups=halves)


def place(source, leaf):
    return ((source ^ leaf) // 4 % 2) * (ROOTS // 2) + source // 8 * 4 + source % 4


def per_device(
    vectors,
    leaf_basis,
    transfer,
    nearfield_source_leaf,
    near_count,
    nearfield_block_matrix,
    far_source,
    far_count,
    far_block,
    top_source,
    top_count,
    top_block,
):
    packed, basis, carried, root, far, top, near_at, near_n, far_at, far_n, top_at = pl.pallas_call(
        coef_kernel,
        out_shape=(
            pltpu.VMEM((PACKED, 32, 128), BF),
            pltpu.VMEM((LEAVES, 32, 128), BF),
            pltpu.VMEM((LEAVES, 32, 32), BF),
            pltpu.VMEM((2 * ROWS, 128), BF),
            pltpu.VMEM((LEAVES, 4, 1024), BF),
            pltpu.VMEM((1, 4, 1024), BF),
            pltpu.VMEM((4, LEAVES), jnp.int32),
            pltpu.VMEM((LEAVES,), jnp.int32),
            pltpu.VMEM((4, LEAVES), jnp.int32),
            pltpu.VMEM((LEAVES,), jnp.int32),
            pltpu.VMEM((1, 4), jnp.int32),
        ),
        in_specs=[HBM] * 10,
        out_specs=(VMEM,) * 11,
        scratch_shapes=[pltpu.VMEM((32, 128), F32), pltpu.SemaphoreType.DMA((10,))],
        name="coefficients",
        **params(1 << 24),
    )(
        stays(vectors),
        stays(leaf_basis),
        stays(transfer),
        stays(far_block),
        stays(top_block),
        stays(nearfield_source_leaf.T),
        stays(near_count),
        stays(far_source.T),
        stays(far_count),
        stays(top_source),
    )

    outside = lax.ppermute(packed, "leaf", [(n, (((n + 1) ^ 1) - 1) % ROOTS) for n in range(ROOTS)])
    inside = lax.ppermute(packed, "leaf", [(n, n ^ 1) for n in range(64)])
    spread = pl.pallas_call(
        spread_kernel,
        out_shape=jax.ShapeDtypeStruct((ROOTS // 4, 2 * ROWS, 128), BF),
        in_specs=[VMEM],
        out_specs=VMEM,
        name="spread",
        **params(1 << 20),
    )(held(root))
    roots = gathered(spread.reshape(ROOTS // 2, ROWS, 128))

    operator = pl.pallas_call(
        top_operator_kernel,
        out_shape=pltpu.VMEM((64, LEAVES * 128), BF),
        in_specs=[VMEM, VMEM],
        out_specs=VMEM,
        name="top_operator",
        **params(1 << 24),
    )(held(carried), held(basis))

    parts = LEAVES // 2
    sent = pltpu.VMEM((parts + 3, 16, 128), BF)
    kept, out1, out2, out3, top_own, names_own = pl.pallas_call(
        near_far_kernel,
        out_shape=(
            pltpu.VMEM((parts, 16, 128), F32),
            sent,
            sent,
            sent,
            pltpu.VMEM((32, 128), BF),
            pltpu.VMEM((ROWS, 128), jnp.int32),
        ),
        in_specs=[VMEM] * 8 + [HBM] + [VMEM] * 3,
        out_specs=(VMEM,) * 6,
        scratch_shapes=[
            pltpu.SMEM((4, LEAVES), jnp.int32),
            pltpu.SMEM((LEAVES,), jnp.int32),
            pltpu.SMEM((4, LEAVES), jnp.int32),
            pltpu.SMEM((LEAVES,), jnp.int32),
            pltpu.SMEM((1, 4), jnp.int32),
            pltpu.VMEM((NONE + 1, 32, 128), BF),
            pltpu.VMEM((NONE + 1, 32, 128), BF),
            pltpu.VMEM((PER_STEP, 32, 128), F32),
            pltpu.VMEM((LEAVES // GROUP, 128, 256), BF),
            pltpu.VMEM((LEAVES, 4, 128, 128), BF),
            pltpu.SemaphoreType.DMA((STEPS + 5,)),
        ],
        name="near_far",
        **params(1 << 30),
    )(
        held(near_at),
        held(near_n),
        held(far_at),
        held(far_n),
        held(top_at),
        held(packed),
        held(outside),
        held(inside),
        stays(nearfield_block_matrix),
        held(far),
        held(top),
        held(basis),
    )

    got = {}
    for k, out in ((2, out2), (1, out1), (3, out3)):
        got[k] = lax.ppermute(out, "level", [(n, n ^ k) for n in range(4)])

    other_roots = lax.ppermute(roots, "leaf", [(n, n ^ 6) for n in range(ROOTS)])

    result = pl.pallas_call(
        final_kernel,
        out_shape=jax.ShapeDtypeStruct((parts, 16, 128), BF),
        in_specs=[SMEM] + [VMEM] * 9,
        out_specs=VMEM,
        name="final",
        **params(1 << 24),
    )(
        top_count,
        held(roots),
        held(other_roots),
        held(operator),
        held(kept),
        held(top_own),
        held(names_own),
        held(got[2]),
        held(got[1]),
        held(got[3]),
    )
    return result.reshape(LEAVES, ROWS, 128)


def solution(mesh):
    placed = (
        P("leaf", None, None),
        P("leaf", None, None),
        P("leaf", None, None),
        P("leaf", "level"),
        P("leaf"),
        P("leaf", "level", None, None),
        P("leaf", "level"),
        P("leaf"),
        P("leaf", "level", None),
        P("leaf", "level"),
        P("leaf"),
        P("leaf", "level", None),
    )
    return jax.shard_map(
        per_device, mesh=mesh, in_specs=placed, out_specs=P("leaf", "level", None), check_vma=False
    )
```

```python
import jax
import jax.numpy as jnp
from jax import lax
from jax.experimental import pallas as pl
from jax.experimental.pallas import tpu as pltpu
from jax.sharding import PartitionSpec as P

BF = jnp.bfloat16
F32 = jnp.float32
LEAVES = 32
ROOTS = 64
GROUP = 4
PACKED = LEAVES + LEAVES // GROUP
ROWS = 8
STEPS = 2
PER_STEP = LEAVES // STEPS
AHEAD = 2
OUTSIDE = [
    (4 * n + k, 4 * n + (k ^ 1) if n in (0, ROOTS - 1) else 4 * (((n + 1) ^ 1) - 1) + k)
    for n in range(ROOTS)
    for k in range(4)
]
NONE = 3 * LEAVES


def dot_nt(a, b):
    return lax.dot_general(a, b, (((1,), (1,)), ((), ())), preferred_element_type=F32)


def dot_nn(a, b):
    return lax.dot_general(a, b, (((1,), (0,)), ((), ())), preferred_element_type=F32)


def two_terms(value):
    high = value.astype(BF)
    return high, (value - high.astype(F32)).astype(BF)


def coef_kernel(
    vectors,
    basis_in,
    transfer_in,
    far_in,
    top_in,
    near_source_in,
    near_count_in,
    far_source_in,
    far_count_in,
    top_source_in,
    packed,
    basis,
    transfer,
    root_out,
    far,
    top,
    near_source,
    near_count,
    far_source,
    far_count,
    top_source,
    wide,
    sems,
):
    pairs = (
        (vectors, packed.at[0:LEAVES]),
        (basis_in, basis),
        (transfer_in, transfer),
        (far_in, far),
        (near_source_in, near_source),
        (near_count_in, near_count),
        (far_source_in, far_source),
        (far_count_in, far_count),
        (top_in, top),
        (top_source_in, top_source),
    )
    copies = [pltpu.make_async_copy(a, b, sems.at[n]) for n, (a, b) in enumerate(pairs)]
    for copy in copies:
        copy.start()
    for copy in copies[:3]:
        copy.wait()
    total = jnp.zeros((32, 32), F32)
    for g in range(LEAVES // GROUP):
        pieces = []
        for m in range(GROUP):
            i = g * GROUP + m
            c = dot_nt(packed[i], basis[i]).astype(BF)
            total = total + dot_nt(c, transfer[i])
            pieces.append(c)
        packed[LEAVES + g] = jnp.concatenate(pieces, axis=1)
    wide[...] = jnp.concatenate([total] * GROUP, axis=1)
    root = wide[pl.ds(pl.multiple_of(lax.axis_index("level") * ROWS, ROWS), ROWS), :].astype(BF)
    root_out[...] = jnp.concatenate([root, root], axis=0)
    for copy in copies[3:]:
        copy.wait()


def spread_kernel(root, spread):
    for t in range(ROOTS // 4):
        spread[t] = root[...]


def couplings(rows4, lane, row):
    x = jnp.concatenate([rows4[:, p * 128 : (p + 1) * 128] for p in range(8)], axis=0)
    out = x
    for d in range(1, 4):
        turned = jnp.where(row < 4 - d, pltpu.roll(x, 32 - d, 0), pltpu.roll(x, 4 - d, 0))
        out = jnp.where((row + d) % 4 == lane, pltpu.roll(turned, 32 * d, 1), out)
    return out


def near_far_kernel(
    near_source_in,
    near_count_in,
    far_source_in,
    far_count_in,
    top_source_in,
    own,
    outside,
    inside,
    blocks_in,
    far,
    top,
    basis,
    kept,
    out1,
    out2,
    out3,
    top_own,
    names_own,
    near_source,
    near_count,
    far_source,
    far_count,
    top_source,
    vtab,
    ctab,
    prod,
    terms,
    blocks,
    sems,
):
    def stream(n):
        part = pl.ds(n * PER_STEP, PER_STEP)
        return pltpu.make_async_copy(blocks_in.at[part], blocks.at[part], sems.at[n])

    small = [
        pltpu.make_async_copy(a, b, sems.at[STEPS + n])
        for n, (a, b) in enumerate(
            (
                (near_source_in, near_source),
                (near_count_in, near_count),
                (far_source_in, far_source),
                (far_count_in, far_count),
                (top_source_in, top_source),
            )
        )
    ]
    for copy in small:
        copy.start()
    for n in range(AHEAD):
        stream(n).start()
    lane = lax.broadcasted_iota(jnp.int32, (32, 128), 1) // 32
    row = lax.broadcasted_iota(jnp.int32, (32, 128), 0) % 4
    me = lax.axis_index("level")
    leaf = lax.axis_index("leaf")
    first = me * 4
    odd = leaf % 2
    for n, part in ((1, own), (2 - 2 * odd, inside), (2 * odd, outside)):
        vtab[pl.ds(n * LEAVES, LEAVES)] = part[0:LEAVES]
        for g in range(LEAVES // GROUP):
            tile = part[LEAVES + g].astype(F32)
            turned = [tile] + [pltpu.roll(tile, 32 * k, 1) for k in range(1, GROUP)]
            for m in range(GROUP):
                v = turned[(0 - m) % GROUP]
                for k in range(1, GROUP):
                    v = jnp.where(lane == k, turned[(k - m) % GROUP], v)
                ctab[n * LEAVES + g * GROUP + m] = v.astype(BF)
    vtab[NONE] = jnp.zeros((32, 128), BF)
    ctab[NONE] = jnp.zeros((32, 128), BF)

    shift = LEAVES - leaf * LEAVES
    for copy in small:
        copy.wait()
    top_f = couplings(top[0].astype(F32), lane, row).astype(BF)
    top_own[...] = top_f
    row8 = lax.broadcasted_iota(jnp.int32, (16, 128), 0)
    names = jnp.zeros((16, 128), jnp.int32)
    for s in range(4):
        names = jnp.where(row8 == s, place(top_source[0, s], leaf), names)
    names_own[...] = names[0:8]
    names = names.astype(F32).astype(BF)
    for out in (out1, out2, out3):
        out[LEAVES // 2] = top_f[0:16]
        out[LEAVES // 2 + 1] = top_f[16:32]
        out[LEAVES // 2 + 2] = names

    same = lax.broadcasted_iota(jnp.int32, (128, 128), 0) // 32 == lax.broadcasted_iota(jnp.int32, (128, 128), 1) // 32
    for g in range(LEAVES // GROUP):
        chosen = []
        matrices = []
        for m in range(GROUP):
            i = g * GROUP + m
            far_at = [jnp.where(first + s < far_count[i], far_source[s, i] + shift, NONE) for s in range(4)]
            c = ctab[far_at[0]]
            for s in range(1, 4):
                c = jnp.where(lane == s, ctab[far_at[s]], c)
            chosen.append(c)
            matrices.append(couplings(far[i].astype(F32), lane, row).astype(BF))
        down = dot_nt(jnp.concatenate(chosen, axis=0), jnp.concatenate(matrices, axis=0))
        terms[g] = jnp.concatenate(two_terms(jnp.where(same, down, 0.0)), axis=1)

    @pl.loop(0, STEPS)
    def _(step):
        stream(step).wait()

        @pl.when(step + AHEAD < STEPS)
        def _():
            stream(step + AHEAD).start()

        for h in range(PER_STEP // GROUP):
            g = step * (PER_STEP // GROUP) + h
            b = basis[pl.ds(g * GROUP, GROUP)].reshape(GROUP * 32, 128)
            value = dot_nn(terms[g], jnp.concatenate([b, b], axis=0))
            for m in range(GROUP):
                i = g * GROUP + m
                near_at = [jnp.where(first + s < near_count[i], near_source[s, i] + shift, NONE) for s in range(4)]
                total = value[m * 32 : m * 32 + 32]
                for s in range(0, 4, 2):
                    lhs = jnp.concatenate([vtab[near_at[s]], vtab[near_at[s + 1]]], axis=1)
                    rhs = jnp.concatenate([blocks[i, s], blocks[i, s + 1]], axis=1)
                    total = total + dot_nt(lhs, rhs)
                prod[h * GROUP + m] = total
            for m in range(0, GROUP, 2):
                pair = (step * PER_STEP + h * GROUP + m) // 2

                def rows(k):
                    at = pl.multiple_of((me ^ k) * ROWS, ROWS)
                    n = h * GROUP + m
                    return jnp.concatenate([prod[n, pl.ds(at, ROWS), :], prod[n + 1, pl.ds(at, ROWS), :]], axis=0)

                kept[pair] = rows(0)
                for k, out in ((1, out1), (2, out2), (3, out3)):
                    out[pair] = rows(k).astype(BF)


def top_operator_kernel(transfer, basis, operator):
    for i in range(LEAVES):
        high, low = two_terms(dot_nn(transfer[i], basis[i]))
        operator[0:32, i * 128 : (i + 1) * 128] = high
        operator[32:64, i * 128 : (i + 1) * 128] = low


def pack_kernel(roots, after, out):
    lane = lax.broadcasted_iota(jnp.int32, (ROWS, 128), 1) // 32
    for n in range(ROOTS // 16):
        halves = []
        for h in range(2):
            v = roots[8 * n + 4 * h].astype(F32)
            for m in range(1, GROUP):
                v = jnp.where(lane == m, roots[8 * n + 4 * h + m].astype(F32), v)
            halves.append(v)
        out[n] = jnp.concatenate(halves, axis=0).astype(BF)


def final_kernel(top_count, roots, other_roots, operator, kept, top_own, names_own, got2, got1, got3, out):
    others = (got1, got2, got3)
    me = lax.axis_index("level")
    tiles = [names_own[...].astype(F32)]
    for got in others:
        tiles.append(got[LEAVES // 2 + 2].astype(F32)[0:ROWS])
    for h in range(LEAVES // 2):
        kept[h] = kept[h] + got1[h].astype(F32) + got2[h].astype(F32) + got3[h].astype(F32)
    lane = lax.broadcasted_iota(jnp.int32, (ROWS, 128), 1) // 32
    total = jnp.zeros((ROWS, 32), F32)
    for k in range(4):
        c = jnp.zeros((ROWS, 128), F32)
        for s in range(4):
            spot = jnp.max(tiles[k][s : s + 1]).astype(jnp.int32)
            index = spot % (ROOTS // 2)
            tile = jnp.where(spot < ROOTS // 2, roots[index // 8].astype(F32), other_roots[index // 8].astype(F32))
            tile = jnp.where(index % 8 < 4, tile[0:ROWS], tile[ROWS : 2 * ROWS])
            tile = pltpu.roll(tile, (s + 4 - index % 4) % 4 * 32, 1)
            live = (me ^ k) * 4 + s < top_count[0]
            c = jnp.where((lane == s) & live, tile, c)
        c = c.astype(BF)
        if k == 0:
            total = total + dot_nt(c, top_own[...])
        else:
            got = others[k - 1]
            total = total + dot_nt(c, jnp.concatenate([got[LEAVES // 2], got[LEAVES // 2 + 1]], axis=0))
    high, low = two_terms(total)
    lhs = jnp.concatenate([high, low, high], axis=1)
    for h in range(LEAVES // 2):
        w = operator[:, h * 256 : (h + 1) * 256]
        t = dot_nn(lhs, jnp.concatenate([w[0:32], w[0:32], w[32:64]], axis=0))
        out[h] = (kept[h] + jnp.concatenate([t[:, 0:128], t[:, 128:256]], axis=0)).astype(BF)


SMEM = pl.BlockSpec(memory_space=pltpu.SMEM)
VMEM = pl.BlockSpec(memory_space=pltpu.VMEM)
HBM = pl.BlockSpec(memory_space=pltpu.HBM)
LIMIT = 16 * 1024 * 1024


def held(value):
    return pltpu.with_memory_space_constraint(value, pltpu.VMEM)


def stays(value):
    return pltpu.with_memory_space_constraint(value, pltpu.HBM)


def params(flops):
    return dict(
        compiler_params=pltpu.CompilerParams(vmem_limit_bytes=LIMIT),
        cost_estimate=pl.CostEstimate(flops=flops, bytes_accessed=1 << 20, transcendentals=0),
    )


def gathered(spread):
    halves = [[n for n in range(ROOTS) if n // 4 % 2 == h] for h in range(2)]
    return lax.all_to_all(spread, "leaf", 0, 0, tiled=True, axis_index_groups=halves)


def place(source, leaf):
    return ((source ^ leaf) // 4 % 2) * (ROOTS // 2) + source // 8 * 4 + source % 4


def per_device(
    vectors,
    leaf_basis,
    transfer,
    nearfield_source_leaf,
    near_count,
    nearfield_block_matrix,
    far_source,
    far_count,
    far_block,
    top_source,
    top_count,
    top_block,
):
    packed, basis, carried, root, far, top, near_at, near_n, far_at, far_n, top_at = pl.pallas_call(
        coef_kernel,
        out_shape=(
            pltpu.VMEM((PACKED, 32, 128), BF),
            pltpu.VMEM((LEAVES, 32, 128), BF),
            pltpu.VMEM((LEAVES, 32, 32), BF),
            pltpu.VMEM((2 * ROWS, 128), BF),
            pltpu.VMEM((LEAVES, 4, 1024), BF),
            pltpu.VMEM((1, 4, 1024), BF),
            pltpu.VMEM((4, LEAVES), jnp.int32),
            pltpu.VMEM((LEAVES,), jnp.int32),
            pltpu.VMEM((4, LEAVES), jnp.int32),
            pltpu.VMEM((LEAVES,), jnp.int32),
            pltpu.VMEM((1, 4), jnp.int32),
        ),
        in_specs=[HBM] * 10,
        out_specs=(VMEM,) * 11,
        scratch_shapes=[pltpu.VMEM((32, 128), F32), pltpu.SemaphoreType.DMA((10,))],
        name="coefficients",
        **params(1 << 24),
    )(
        stays(vectors),
        stays(leaf_basis),
        stays(transfer),
        stays(far_block),
        stays(top_block),
        stays(nearfield_source_leaf.T),
        stays(near_count),
        stays(far_source.T),
        stays(far_count),
        stays(top_source),
    )

    outside = lax.ppermute(packed, ("leaf", "level"), OUTSIDE)
    inside = lax.ppermute(packed, "leaf", [(n, n ^ 1) for n in range(64)])
    spread = pl.pallas_call(
        spread_kernel,
        out_shape=jax.ShapeDtypeStruct((ROOTS // 4, 2 * ROWS, 128), BF),
        in_specs=[VMEM],
        out_specs=VMEM,
        name="spread",
        **params(1 << 20),
    )(held(root))
    roots = gathered(spread.reshape(ROOTS // 2, ROWS, 128))

    operator = pl.pallas_call(
        top_operator_kernel,
        out_shape=pltpu.VMEM((64, LEAVES * 128), BF),
        in_specs=[VMEM, VMEM],
        out_specs=VMEM,
        name="top_operator",
        **params(1 << 24),
    )(held(carried), held(basis))

    parts = LEAVES // 2
    sent = pltpu.VMEM((parts + 3, 16, 128), BF)
    kept, out1, out2, out3, top_own, names_own = pl.pallas_call(
        near_far_kernel,
        out_shape=(
            pltpu.VMEM((parts, 16, 128), F32),
            sent,
            sent,
            sent,
            pltpu.VMEM((32, 128), BF),
            pltpu.VMEM((ROWS, 128), jnp.int32),
        ),
        in_specs=[VMEM] * 8 + [HBM] + [VMEM] * 3,
        out_specs=(VMEM,) * 6,
        scratch_shapes=[
            pltpu.SMEM((4, LEAVES), jnp.int32),
            pltpu.SMEM((LEAVES,), jnp.int32),
            pltpu.SMEM((4, LEAVES), jnp.int32),
            pltpu.SMEM((LEAVES,), jnp.int32),
            pltpu.SMEM((1, 4), jnp.int32),
            pltpu.VMEM((NONE + 1, 32, 128), BF),
            pltpu.VMEM((NONE + 1, 32, 128), BF),
            pltpu.VMEM((PER_STEP, 32, 128), F32),
            pltpu.VMEM((LEAVES // GROUP, 128, 256), BF),
            pltpu.VMEM((LEAVES, 4, 128, 128), BF),
            pltpu.SemaphoreType.DMA((STEPS + 5,)),
        ],
        name="near_far",
        **params(1 << 30),
    )(
        held(near_at),
        held(near_n),
        held(far_at),
        held(far_n),
        held(top_at),
        held(packed),
        held(outside),
        held(inside),
        stays(nearfield_block_matrix),
        held(far),
        held(top),
        held(basis),
    )

    got = {}
    for k, out in ((2, out2), (1, out1), (3, out3)):
        got[k] = lax.ppermute(out, "level", [(n, n ^ k) for n in range(4)])

    roots = pl.pallas_call(
        pack_kernel,
        out_shape=pltpu.VMEM((ROOTS // 16, 2 * ROWS, 128), BF),
        in_specs=[VMEM] * 2,
        out_specs=VMEM,
        name="pack",
        **params(1 << 20),
    )(held(roots), held(names_own))
    other_roots = lax.ppermute(roots, "leaf", [(n, n ^ 6) for n in range(ROOTS)])

    result = pl.pallas_call(
        final_kernel,
        out_shape=jax.ShapeDtypeStruct((parts, 16, 128), BF),
        in_specs=[SMEM] + [VMEM] * 9,
        out_specs=VMEM,
        name="final",
        **params(1 << 24),
    )(
        top_count,
        held(roots),
        held(other_roots),
        held(operator),
        held(kept),
        held(top_own),
        held(names_own),
        held(got[2]),
        held(got[1]),
        held(got[3]),
    )
    return result.reshape(LEAVES, ROWS, 128)


def solution(mesh):
    placed = (
        P("leaf", None, None),
        P("leaf", None, None),
        P("leaf", None, None),
        P("leaf", "level"),
        P("leaf"),
        P("leaf", "level", None, None),
        P("leaf", "level"),
        P("leaf"),
        P("leaf", "level", None),
        P("leaf", "level"),
        P("leaf"),
        P("leaf", "level", None),
    )
    return jax.shard_map(
        per_device, mesh=mesh, in_specs=placed, out_specs=P("leaf", "level", None), check_vma=False
    )
```

```python
import jax
import jax.numpy as jnp
from jax import lax
from jax.experimental import pallas as pl
from jax.experimental.pallas import tpu as pltpu
from jax.sharding import PartitionSpec as P

BF = jnp.bfloat16
F32 = jnp.float32
LEAVES = 32
ROOTS = 64
GROUP = 4
PACKED = LEAVES + LEAVES // GROUP
ROWS = 8
STEPS = 2
PER_STEP = LEAVES // STEPS
AHEAD = 2
OUTSIDE = [
    (4 * n + k, 4 * n + (k ^ 1) if n in (0, ROOTS - 1) else 4 * (((n + 1) ^ 1) - 1) + k)
    for n in range(ROOTS)
    for k in range(4)
]
NONE = 3 * LEAVES


def dot_nt(a, b):
    return lax.dot_general(a, b, (((1,), (1,)), ((), ())), preferred_element_type=F32)


def dot_nn(a, b):
    return lax.dot_general(a, b, (((1,), (0,)), ((), ())), preferred_element_type=F32)


def two_terms(value):
    high = value.astype(BF)
    return high, (value - high.astype(F32)).astype(BF)


def coef_kernel(
    vectors,
    basis_in,
    transfer_in,
    far_in,
    top_in,
    near_source_in,
    near_count_in,
    far_source_in,
    far_count_in,
    top_source_in,
    packed,
    basis,
    transfer,
    root_out,
    far,
    top,
    near_source,
    near_count,
    far_source,
    far_count,
    top_source,
    wide,
    sems,
):
    pairs = (
        (vectors, packed.at[0:LEAVES]),
        (basis_in, basis),
        (transfer_in, transfer),
        (far_in, far),
        (near_source_in, near_source),
        (near_count_in, near_count),
        (far_source_in, far_source),
        (far_count_in, far_count),
        (top_in, top),
        (top_source_in, top_source),
    )
    copies = [pltpu.make_async_copy(a, b, sems.at[n]) for n, (a, b) in enumerate(pairs)]
    for copy in copies:
        copy.start()
    for copy in copies[:3]:
        copy.wait()
    total = jnp.zeros((32, 32), F32)
    for g in range(LEAVES // GROUP):
        pieces = []
        for m in range(GROUP):
            i = g * GROUP + m
            c = dot_nt(packed[i], basis[i]).astype(BF)
            total = total + dot_nt(c, transfer[i])
            pieces.append(c)
        packed[LEAVES + g] = jnp.concatenate(pieces, axis=1)
    wide[...] = jnp.concatenate([total] * GROUP, axis=1)
    root = wide[pl.ds(pl.multiple_of(lax.axis_index("level") * ROWS, ROWS), ROWS), :].astype(BF)
    root_out[...] = jnp.concatenate([root, root], axis=0)
    for copy in copies[3:]:
        copy.wait()


def spread_kernel(root, spread):
    for t in range(ROOTS // 4):
        spread[t] = root[...]


def couplings(rows4, lane, row):
    x = jnp.concatenate([rows4[:, p * 128 : (p + 1) * 128] for p in range(8)], axis=0)
    out = x
    for d in range(1, 4):
        turned = jnp.where(row < 4 - d, pltpu.roll(x, 32 - d, 0), pltpu.roll(x, 4 - d, 0))
        out = jnp.where((row + d) % 4 == lane, pltpu.roll(turned, 32 * d, 1), out)
    return out


def near_far_kernel(
    near_source_in,
    near_count_in,
    far_source_in,
    far_count_in,
    top_source_in,
    own,
    outside,
    inside,
    blocks_in,
    far,
    top,
    basis,
    kept,
    out1,
    out2,
    out3,
    top_own,
    names_own,
    near_source,
    near_count,
    far_source,
    far_count,
    top_source,
    vtab,
    ctab,
    prod,
    terms,
    blocks,
    sems,
):
    def stream(n):
        part = pl.ds(n * PER_STEP, PER_STEP)
        return pltpu.make_async_copy(blocks_in.at[part], blocks.at[part], sems.at[n])

    small = [
        pltpu.make_async_copy(a, b, sems.at[STEPS + n])
        for n, (a, b) in enumerate(
            (
                (near_source_in, near_source),
                (near_count_in, near_count),
                (far_source_in, far_source),
                (far_count_in, far_count),
                (top_source_in, top_source),
            )
        )
    ]
    for copy in small:
        copy.start()
    for n in range(AHEAD):
        stream(n).start()
    lane = lax.broadcasted_iota(jnp.int32, (32, 128), 1) // 32
    row = lax.broadcasted_iota(jnp.int32, (32, 128), 0) % 4
    me = lax.axis_index("level")
    leaf = lax.axis_index("leaf")
    first = me * 4
    odd = leaf % 2
    for n, part in ((1, own), (2 - 2 * odd, inside), (2 * odd, outside)):
        vtab[pl.ds(n * LEAVES, LEAVES)] = part[0:LEAVES]
        for g in range(LEAVES // GROUP):
            tile = part[LEAVES + g].astype(F32)
            turned = [tile] + [pltpu.roll(tile, 32 * k, 1) for k in range(1, GROUP)]
            for m in range(GROUP):
                v = turned[(0 - m) % GROUP]
                for k in range(1, GROUP):
                    v = jnp.where(lane == k, turned[(k - m) % GROUP], v)
                ctab[n * LEAVES + g * GROUP + m] = v.astype(BF)
    vtab[NONE] = jnp.zeros((32, 128), BF)
    ctab[NONE] = jnp.zeros((32, 128), BF)

    shift = LEAVES - leaf * LEAVES
    for copy in small:
        copy.wait()
    top_f = couplings(top[0].astype(F32), lane, row).astype(BF)
    top_own[...] = top_f
    row8 = lax.broadcasted_iota(jnp.int32, (16, 128), 0)
    names = jnp.zeros((16, 128), jnp.int32)
    for s in range(4):
        names = jnp.where(row8 == s, place(top_source[0, s], leaf), names)
    names_own[...] = names[0:8]
    names = names.astype(F32).astype(BF)
    for out in (out1, out2, out3):
        out[LEAVES // 2] = top_f[0:16]
        out[LEAVES // 2 + 1] = top_f[16:32]
        out[LEAVES // 2 + 2] = names

    same = lax.broadcasted_iota(jnp.int32, (128, 128), 0) // 32 == lax.broadcasted_iota(jnp.int32, (128, 128), 1) // 32
    for g in range(LEAVES // GROUP):
        chosen = []
        matrices = []
        for m in range(GROUP):
            i = g * GROUP + m
            far_at = [jnp.where(first + s < far_count[i], far_source[s, i] + shift, NONE) for s in range(4)]
            c = ctab[far_at[0]]
            for s in range(1, 4):
                c = jnp.where(lane == s, ctab[far_at[s]], c)
            chosen.append(c)
            matrices.append(couplings(far[i].astype(F32), lane, row).astype(BF))
        down = dot_nt(jnp.concatenate(chosen, axis=0), jnp.concatenate(matrices, axis=0))
        terms[g] = jnp.concatenate(two_terms(jnp.where(same, down, 0.0)), axis=1)

    @pl.loop(0, STEPS)
    def _(step):
        stream(step).wait()

        @pl.when(step + AHEAD < STEPS)
        def _():
            stream(step + AHEAD).start()

        for h in range(PER_STEP // GROUP):
            g = step * (PER_STEP // GROUP) + h
            b = basis[pl.ds(g * GROUP, GROUP)].reshape(GROUP * 32, 128)
            value = dot_nn(terms[g], jnp.concatenate([b, b], axis=0))
            for m in range(GROUP):
                i = g * GROUP + m
                near_at = [jnp.where(first + s < near_count[i], near_source[s, i] + shift, NONE) for s in range(4)]
                total = value[m * 32 : m * 32 + 32]
                for s in range(0, 4, 2):
                    lhs = jnp.concatenate([vtab[near_at[s]], vtab[near_at[s + 1]]], axis=1)
                    rhs = jnp.concatenate([blocks[i, s], blocks[i, s + 1]], axis=1)
                    total = total + dot_nt(lhs, rhs)
                prod[h * GROUP + m] = total
            for m in range(0, GROUP, 2):
                pair = (step * PER_STEP + h * GROUP + m) // 2

                def rows(k):
                    at = pl.multiple_of((me ^ k) * ROWS, ROWS)
                    n = h * GROUP + m
                    return jnp.concatenate([prod[n, pl.ds(at, ROWS), :], prod[n + 1, pl.ds(at, ROWS), :]], axis=0)

                kept[pair] = rows(0)
                for k, out in ((1, out1), (2, out2), (3, out3)):
                    out[pair] = rows(k).astype(BF)


def top_operator_kernel(transfer, basis, operator):
    for i in range(LEAVES):
        high, low = two_terms(dot_nn(transfer[i], basis[i]))
        operator[0:32, i * 128 : (i + 1) * 128] = high
        operator[32:64, i * 128 : (i + 1) * 128] = low


def pack_kernel(roots, after, out):
    lane = lax.broadcasted_iota(jnp.int32, (ROWS, 128), 1) // 32
    for n in range(ROOTS // 16):
        halves = []
        for h in range(2):
            v = roots[8 * n + 4 * h].astype(F32)
            for m in range(1, GROUP):
                v = jnp.where(lane == m, roots[8 * n + 4 * h + m].astype(F32), v)
            halves.append(v)
        out[n] = jnp.concatenate(halves, axis=0).astype(BF)


def final_kernel(top_count, roots, other_roots, operator, kept, top_own, names_own, got2, got3, got1, out):
    others = (got1, got2, got3)
    me = lax.axis_index("level")
    tiles = [names_own[...].astype(F32)]
    for got in others:
        tiles.append(got[LEAVES // 2 + 2].astype(F32)[0:ROWS])
    for h in range(LEAVES // 2):
        kept[h] = kept[h] + got1[h].astype(F32) + got2[h].astype(F32) + got3[h].astype(F32)
    lane = lax.broadcasted_iota(jnp.int32, (ROWS, 128), 1) // 32
    total = jnp.zeros((ROWS, 32), F32)
    for k in range(4):
        c = jnp.zeros((ROWS, 128), F32)
        for s in range(4):
            spot = jnp.max(tiles[k][s : s + 1]).astype(jnp.int32)
            index = spot % (ROOTS // 2)
            tile = jnp.where(spot < ROOTS // 2, roots[index // 8].astype(F32), other_roots[index // 8].astype(F32))
            tile = jnp.where(index % 8 < 4, tile[0:ROWS], tile[ROWS : 2 * ROWS])
            tile = pltpu.roll(tile, (s + 4 - index % 4) % 4 * 32, 1)
            live = (me ^ k) * 4 + s < top_count[0]
            c = jnp.where((lane == s) & live, tile, c)
        c = c.astype(BF)
        if k == 0:
            total = total + dot_nt(c, top_own[...])
        else:
            got = others[k - 1]
            total = total + dot_nt(c, jnp.concatenate([got[LEAVES // 2], got[LEAVES // 2 + 1]], axis=0))
    high, low = two_terms(total)
    lhs = jnp.concatenate([high, low, high], axis=1)
    for h in range(LEAVES // 2):
        w = operator[:, h * 256 : (h + 1) * 256]
        t = dot_nn(lhs, jnp.concatenate([w[0:32], w[0:32], w[32:64]], axis=0))
        out[h] = (kept[h] + jnp.concatenate([t[:, 0:128], t[:, 128:256]], axis=0)).astype(BF)


SMEM = pl.BlockSpec(memory_space=pltpu.SMEM)
VMEM = pl.BlockSpec(memory_space=pltpu.VMEM)
HBM = pl.BlockSpec(memory_space=pltpu.HBM)
LIMIT = 16 * 1024 * 1024


def held(value):
    return pltpu.with_memory_space_constraint(value, pltpu.VMEM)


def stays(value):
    return pltpu.with_memory_space_constraint(value, pltpu.HBM)


def params(flops):
    return dict(
        compiler_params=pltpu.CompilerParams(vmem_limit_bytes=LIMIT),
        cost_estimate=pl.CostEstimate(flops=flops, bytes_accessed=1 << 20, transcendentals=0),
    )


def gathered(spread):
    halves = [[n for n in range(ROOTS) if n // 4 % 2 == h] for h in range(2)]
    return lax.all_to_all(spread, "leaf", 0, 0, tiled=True, axis_index_groups=halves)


def place(source, leaf):
    return ((source ^ leaf) // 4 % 2) * (ROOTS // 2) + source // 8 * 4 + source % 4


def per_device(
    vectors,
    leaf_basis,
    transfer,
    nearfield_source_leaf,
    near_count,
    nearfield_block_matrix,
    far_source,
    far_count,
    far_block,
    top_source,
    top_count,
    top_block,
):
    packed, basis, carried, root, far, top, near_at, near_n, far_at, far_n, top_at = pl.pallas_call(
        coef_kernel,
        out_shape=(
            pltpu.VMEM((PACKED, 32, 128), BF),
            pltpu.VMEM((LEAVES, 32, 128), BF),
            pltpu.VMEM((LEAVES, 32, 32), BF),
            pltpu.VMEM((2 * ROWS, 128), BF),
            pltpu.VMEM((LEAVES, 4, 1024), BF),
            pltpu.VMEM((1, 4, 1024), BF),
            pltpu.VMEM((4, LEAVES), jnp.int32),
            pltpu.VMEM((LEAVES,), jnp.int32),
            pltpu.VMEM((4, LEAVES), jnp.int32),
            pltpu.VMEM((LEAVES,), jnp.int32),
            pltpu.VMEM((1, 4), jnp.int32),
        ),
        in_specs=[HBM] * 10,
        out_specs=(VMEM,) * 11,
        scratch_shapes=[pltpu.VMEM((32, 128), F32), pltpu.SemaphoreType.DMA((10,))],
        name="coefficients",
        **params(1 << 24),
    )(
        stays(vectors),
        stays(leaf_basis),
        stays(transfer),
        stays(far_block),
        stays(top_block),
        stays(nearfield_source_leaf.T),
        stays(near_count),
        stays(far_source.T),
        stays(far_count),
        stays(top_source),
    )

    outside = lax.ppermute(packed, ("leaf", "level"), OUTSIDE)
    inside = lax.ppermute(packed, "leaf", [(n, n ^ 1) for n in range(64)])
    spread = pl.pallas_call(
        spread_kernel,
        out_shape=jax.ShapeDtypeStruct((ROOTS // 4, 2 * ROWS, 128), BF),
        in_specs=[VMEM],
        out_specs=VMEM,
        name="spread",
        **params(1 << 20),
    )(held(root))
    roots = gathered(spread.reshape(ROOTS // 2, ROWS, 128))

    operator = pl.pallas_call(
        top_operator_kernel,
        out_shape=pltpu.VMEM((64, LEAVES * 128), BF),
        in_specs=[VMEM, VMEM],
        out_specs=VMEM,
        name="top_operator",
        **params(1 << 24),
    )(held(carried), held(basis))

    parts = LEAVES // 2
    sent = pltpu.VMEM((parts + 3, 16, 128), BF)
    kept, out1, out2, out3, top_own, names_own = pl.pallas_call(
        near_far_kernel,
        out_shape=(
            pltpu.VMEM((parts, 16, 128), F32),
            sent,
            sent,
            sent,
            pltpu.VMEM((32, 128), BF),
            pltpu.VMEM((ROWS, 128), jnp.int32),
        ),
        in_specs=[VMEM] * 8 + [HBM] + [VMEM] * 3,
        out_specs=(VMEM,) * 6,
        scratch_shapes=[
            pltpu.SMEM((4, LEAVES), jnp.int32),
            pltpu.SMEM((LEAVES,), jnp.int32),
            pltpu.SMEM((4, LEAVES), jnp.int32),
            pltpu.SMEM((LEAVES,), jnp.int32),
            pltpu.SMEM((1, 4), jnp.int32),
            pltpu.VMEM((NONE + 1, 32, 128), BF),
            pltpu.VMEM((NONE + 1, 32, 128), BF),
            pltpu.VMEM((PER_STEP, 32, 128), F32),
            pltpu.VMEM((LEAVES // GROUP, 128, 256), BF),
            pltpu.VMEM((LEAVES, 4, 128, 128), BF),
            pltpu.SemaphoreType.DMA((STEPS + 5,)),
        ],
        name="near_far",
        **params(1 << 30),
    )(
        held(near_at),
        held(near_n),
        held(far_at),
        held(far_n),
        held(top_at),
        held(packed),
        held(outside),
        held(inside),
        stays(nearfield_block_matrix),
        held(far),
        held(top),
        held(basis),
    )

    got = {}
    for k, out in ((2, out2), (3, out3), (1, out1)):
        got[k] = lax.ppermute(out, "level", [(n, n ^ k) for n in range(4)])

    roots = pl.pallas_call(
        pack_kernel,
        out_shape=pltpu.VMEM((ROOTS // 16, 2 * ROWS, 128), BF),
        in_specs=[VMEM] * 2,
        out_specs=VMEM,
        name="pack",
        **params(1 << 20),
    )(held(roots), held(names_own))
    other_roots = lax.ppermute(roots, "leaf", [(n, n ^ 6) for n in range(ROOTS)])

    result = pl.pallas_call(
        final_kernel,
        out_shape=jax.ShapeDtypeStruct((parts, 16, 128), BF),
        in_specs=[SMEM] + [VMEM] * 9,
        out_specs=VMEM,
        name="final",
        **params(1 << 24),
    )(
        top_count,
        held(roots),
        held(other_roots),
        held(operator),
        held(kept),
        held(top_own),
        held(names_own),
        held(got[2]),
        held(got[3]),
        held(got[1]),
    )
    return result.reshape(LEAVES, ROWS, 128)


def solution(mesh):
    placed = (
        P("leaf", None, None),
        P("leaf", None, None),
        P("leaf", None, None),
        P("leaf", "level"),
        P("leaf"),
        P("leaf", "level", None, None),
        P("leaf", "level"),
        P("leaf"),
        P("leaf", "level", None),
        P("leaf", "level"),
        P("leaf"),
        P("leaf", "level", None),
    )
    return jax.shard_map(
        per_device, mesh=mesh, in_specs=placed, out_specs=P("leaf", "level", None), check_vma=False
    )
```
